512 devices in a mesh: section: 16 (over z), tensor: 16 (over x, y_hi, core), dp: 2 (over y_lo).
Axes of the slice: x: 4, y: 4 (y_hi: 2, y_lo: 2; y = y_hi * 2 + y_lo), z: 16, core: 2. Of those that a mesh axis runs over, the one named last changes fastest.
Arguments:
- enc_out: float32 [2, 384, 4096], P('dp', 'tensor'), may hold values from -6 to 6
- gain: float32 [4096], replicated, may hold values from 0.5 to 1.5
- weights: bfloat16 [16, 4096, 4096], P('section', None, 'tensor'), may hold values from -0.09375 to 0.09375
- kv_grad: bfloat16 [16, 2, 384, 4096], P('section', 'dp', None, 'tensor'), may hold values from -4 to 4
Outputs:
- weight_grad: bfloat16 [16, 4096, 4096], P('section', None, 'tensor')
- enc_grad: bfloat16 [2, 384, 4096], P('dp', 'tensor', 'section')
The draws below stay inside these ranges and needn't reach their ends.
All inputs are finite; a program needn't handle non-finite values.
Results may differ from the reference program's by a relative error of at most 0.025.
Values may be sent and summed in bfloat16 or wider, within the bound.
A program may use at most 64 MiB of HBM per device.

```python
import jax
import jax.numpy as jnp
from jax import lax

D = 4096
TOK = 384
HDK = 4096
N_SECTION = 16
N_TENSOR = 16
N_DP = 2


def shard_levels(own_key, dims, cuts, least, high):
    factor_of = 1.0
    for dim, parts in cuts:
        heights = jax.random.uniform(jax.random.fold_in(jax.random.fold_in(own_key, 6), dim), (parts,), jnp.float32, least / len(cuts), high / len(cuts))
        factor_of = factor_of * jnp.repeat(jnp.exp(heights), dims[dim] // parts).reshape((-1,) + (1,) * (len(dims) - 1 - dim))
    return factor_of


def gaussian(key, dims, spread, most, split=(), kind=jnp.bfloat16):
    drawn = spread * jax.random.normal(key, dims, jnp.float32)
    if split:
        drawn = drawn * shard_levels(key, dims, split, -0.22, 0.18)
    return jnp.clip(drawn, -most, most).astype(kind)


def setup_inputs(seed: int = 0) -> dict:
    key_of = jax.random.split(jax.random.key(seed), 5)
    enc_out = gaussian(key_of[0], (N_DP, TOK, D), 1.0, 6.0, ((0, 2), (1, 16)), jnp.float32)
    gain = jnp.clip(1.0 + 0.1 * jax.random.normal(key_of[1], (D,), jnp.float32), 0.5, 1.5)
    weights = gaussian(key_of[2], (N_SECTION, D, HDK), D ** -0.5, 0.09375, ((0, 16), (2, 16)))
    kv_grad = gaussian(key_of[3], (N_SECTION, N_DP, TOK, HDK), 0.3, 4.0, ((0, 16), (1, 2), (3, 16)))
    return {"enc_out": enc_out, "gain": gain, "weights": weights, "kv_grad": kv_grad}


def reference(enc_out, gain, weights, kv_grad):
    inv_rms = lax.rsqrt(lax.optimization_barrier(jnp.mean(enc_out * enc_out, axis=-1, keepdims=True)) + 1e-06)
    normed = enc_out * inv_rms
    memory = (normed * gain).astype(jnp.bfloat16)
    mem_f32 = memory.astype(jnp.float32)
    enc_sections = N_SECTION // 4

    def weight_term(section_id):
        grads = kv_grad[section_id].astype(jnp.float32)
        per_rep = jnp.einsum('bxd,bxh->bdh', mem_f32, grads)
        rounded = lax.optimization_barrier(per_rep.astype(jnp.bfloat16)).astype(jnp.float32)
        summed = lax.optimization_barrier(jnp.sum(rounded, axis=0))
        active = (section_id >= enc_sections).astype(jnp.float32)
        return (summed * active).astype(jnp.bfloat16)
    weight_grad = lax.map(weight_term, jnp.arange(N_SECTION, dtype=jnp.int32))
    group = HDK // N_TENSOR

    def section_term(section_id, summed):
        grads = kv_grad[section_id].astype(jnp.float32).reshape(N_DP, TOK, N_TENSOR, group)
        wts = weights[section_id].astype(jnp.float32).reshape(D, N_TENSOR, group)
        part = jnp.einsum('bxtc,dtc->btxd', grads, wts)
        rounded = lax.optimization_barrier(part.astype(jnp.bfloat16)).astype(jnp.float32)
        return summed + lax.optimization_barrier(jnp.sum(rounded, axis=1))
    memory_grad = lax.fori_loop(enc_sections, N_SECTION, section_term, jnp.zeros((N_DP, TOK, D), jnp.float32))
    scaled = gain * memory_grad
    row_dot = lax.optimization_barrier(jnp.mean(normed * scaled, axis=-1, keepdims=True))
    enc_grad = (inv_rms * (scaled - normed * row_dot)).astype(jnp.bfloat16)
    return (weight_grad, enc_grad)
```

```python
import functools

import jax
import jax.numpy as jnp
from jax import lax
from jax.experimental import pallas as pl
from jax.experimental.pallas import tpu as pltpu
from jax.sharding import PartitionSpec as P

F32, BF16 = jnp.float32, jnp.bfloat16
X, Y = 4, 4
NT = (((1,), (1,)), ((), ()))
TN = (((0,), (0,)), ((), ()))


def kernel(
    nz,
    enc_ref,
    gain_ref,
    w_ref,
    kv_ref,
    wg_ref,
    eg_ref,
    xs,
    xr,
    mem,
    kvs,
    ws,
    first,
    run,
    gs,
    gr,
    hs,
    hr,
    ow,
    loc_sem,
    x_sem,
    kv_sem,
    w_ss,
    w_rs,
    ag_ss,
    ag_rs,
    z_ss,
    z_rs,
    t_ss,
    t_rs,
    h_ss,
    h_rs,
    o_sem,
):
    z, t, b = lax.axis_index("section"), lax.axis_index("tensor"), lax.axis_index("dp")
    x, yh, c = t // 4, (t // 2) % 2, t % 2
    y = yh * 2 + b
    o = 1 - c
    nt = X * 4
    rows, width = enc_ref.shape
    half = nz // 2
    cols = half * 128
    tok = kvs.shape[2]
    sub = tok // 2
    act = (z >= nz // 4).astype(F32)

    def dev(x_, y_, z_, c_):
        return (z_, x_ * 4 + (y_ // 2) * 2 + c_, y_ % 2)

    def remote(src, dst, ss, rs, to):
        return pltpu.make_async_remote_copy(
            src_ref=src,
            dst_ref=dst,
            send_sem=ss,
            recv_sem=rs,
            device_id=to,
            device_id_type=pl.DeviceIdType.MESH,
        )

    me = dev(x, y, z, c)
    other = dev(x, y, z, o)
    sent = []

    def send(src, dst, ss, rs, to):
        copy = remote(src, dst, ss, rs, to)
        copy.start()
        sent.append(copy)

    def arrived(dst, ss, rs):
        remote(dst, dst, ss, rs, other).wait_recv()

    kv_load = pltpu.make_async_copy(kv_ref, kvs.at[c, b], loc_sem.at[0])
    kv_load.start()
    w_load = pltpu.make_async_copy(w_ref.at[:, c], ws.at[c], loc_sem.at[1])
    w_load.start()

    barrier = pltpu.get_barrier_semaphore()

    def greet(to):
        pl.semaphore_signal(barrier, inc=1, device_id=to, device_id_type=pl.DeviceIdType.MESH)

    for i in range(1, nt):
        greet((z, lax.rem(t + i, nt), b))
    for i in range(1, nz):
        greet((lax.rem(z + i, nz), t, b))
    greet(dev(x, (y + 1) % Y, z, c))
    greet(dev(x, (y + 3) % Y, z, c))

    enc = enc_ref[...]
    inv = lax.rsqrt(jnp.mean(enc * enc, axis=1, keepdims=True) + 1e-06)
    own_cols = []
    for s in range(nz):
        part = (enc[:, s * 256 : (s + 1) * 256] * inv) * gain_ref[:, s * 256 : (s + 1) * 256]
        lo, hi = part[:, :128], part[:, 128:]
        own_cols.append(jnp.where(c == 0, lo, hi))
        xs[:, s * 128 : (s + 1) * 128] = jnp.where(c == 0, hi, lo).astype(BF16)

    pl.semaphore_wait(barrier, nt - 1 + nz - 1 + 2)

    send(xs, xr, x_sem.at[0], x_sem.at[1], other)
    kv_load.wait()
    send(kvs.at[c, b], kvs.at[c, b], kv_sem.at[0], kv_sem.at[1], other)
    order = [half]
    for m in range(half - 1, 0, -1):
        order += [m, nz - m]
    order += [0]
    for m in order:
        d = lax.rem(z + m, nz)
        send(w_ref.at[d, o], ws.at[c, d], w_ss.at[d], w_rs.at[d], other)
    dp_peer = dev(x, yh * 2 + (1 - b), z, c)

    def at_xy(h, f, g):
        return (f, g) if h == 0 else (g, f)

    def slot(h, f, g):
        x_, y_ = at_xy(h, f, g)
        return mem.at[h, y_ % 2, x_, y_ // 2]

    def place(h, f, g):
        x_, y_ = at_xy(h, f, g)
        return dev(x_, y_, z, c)

    fg = [(x, y), (y, x)]
    half_cols = (pl.ds(0, cols // 2), pl.ds(cols // 2, cols // 2))

    def sems(h, k):
        return ag_ss.at[h, k], ag_rs.at[h, k]

    STEP = (1, 3)

    def second(h, i):
        f, g = fg[h]
        f_ = (f + (0, 3, 1, 2)[i]) % 4
        for d in range(2):
            s = slot(h, f_, g)
            send(s, s, *sems(h, 4 + 2 * i + d), place(h, f, (g + STEP[d]) % 4))

    def gather0(h):
        f, g = fg[h]
        s = slot(h, f, g)
        for d in range(2):
            send(s, s, *sems(h, d), place(h, (f + STEP[d]) % 4, g))
        second(h, 0)

    def gather1(h):
        f, g = fg[h]
        for d in range(2):
            s = slot(h, (f + STEP[1 - d]) % 4, g)
            arrived(s, *sems(h, d))
            s = s.at[:, half_cols[d]]
            send(s, s, *sems(h, 2 + d), place(h, (f + STEP[d]) % 4, g))
        second(h, 1)
        second(h, 2)

    def gather2(h):
        f, g = fg[h]
        for d in range(2):
            arrived(slot(h, (f + 2) % 4, g).at[:, half_cols[d]], *sems(h, 2 + d))
        second(h, 3)

    def gather3(h, i):
        f, g = fg[h]
        f_ = (f + (0, 3, 1, 2)[i]) % 4
        for d in range(2):
            s = slot(h, f_, (g + STEP[1 - d]) % 4)
            arrived(s, *sems(h, 4 + 2 * i + d))
            s = s.at[:, half_cols[d]]
            send(s, s, *sems(h, 12 + 2 * i + d), place(h, f, (g + STEP[d]) % 4))

    def gather4(h):
        f, g = fg[h]
        for i in range(4):
            f_ = (f + (0, 3, 1, 2)[i]) % 4
            for d in range(2):
                s = slot(h, f_, (g + 2) % 4).at[:, half_cols[d]]
                arrived(s, *sems(h, 12 + 2 * i + d))

    arrived(xr, x_sem.at[0], x_sem.at[1])
    for h in range(2):
        for s in range(half):
            mine = own_cols[h * half + s]
            theirs = xr[:, (h * half + s) * 128 : (h * half + s + 1) * 128].astype(F32)
            both = jnp.concatenate(
                [jnp.where(c == 0, mine, theirs), jnp.where(c == 0, theirs, mine)], axis=0
            )
            mem[h, b, x, yh, :, s * 128 : (s + 1) * 128] = both.astype(BF16)
        gather0(h)
    send(kvs.at[c, b], kvs.at[c, b], kv_sem.at[2], kv_sem.at[3], dp_peer)

    w_load.wait()
    arrived(kvs.at[o, b], kv_sem.at[0], kv_sem.at[1])

    def term(d):
        arrived(ws.at[o, d], w_ss.at[d], w_rs.at[d])
        out = lax.dot_general(kvs[0, b], ws[0, d], NT, preferred_element_type=F32)
        out += lax.dot_general(kvs[1, b], ws[1, d], NT, preferred_element_type=F32)
        return out * act

    def z_step(m):
        to_up = term(lax.rem(z + m, nz))
        to_down = to_up if 2 * m == nz else term(lax.rem(z + nz - m, nz))
        for j in range(2):
            for d in range(2):
                if m == half and d != j:
                    continue
                mine = (to_up, to_down)[d][j * sub : (j + 1) * sub]
                if m == half or (m == half - 1 and d != j):
                    src = first.at[d, j]
                    src[...] = mine.astype(BF16)
                else:
                    src = run.at[d, j, m]
                    arrived(src, z_ss.at[d, j, m], z_rs.at[d, j, m])
                    src[...] = (src[...].astype(F32) + mine).astype(BF16)
                to = dev(x, y, lax.rem(z + (1, nz - 1)[d], nz), c)
                send(src, run.at[d, j, m - 1], z_ss.at[d, j, m - 1], z_rs.at[d, j, m - 1], to)

    def kv_forward():
        got = kvs.at[c, 1 - b]
        arrived(got, kv_sem.at[2], kv_sem.at[3])
        send(got, got, kv_sem.at[4], kv_sem.at[5], other)

    def both(f, *args):
        for h in range(2):
            f(h, *args)

    events = {
        half - 1: [lambda: both(gather1)],
        half - 2: [lambda: both(gather2), lambda: both(gather3, 0), kv_forward],
        half - 4: [lambda: both(gather3, 1), lambda: both(gather3, 2)],
        half - 5: [lambda: both(gather3, 3)],
    }
    for m in range(half, 0, -1):
        z_step(m)
        for event in events.get(m, ()):
            event()

    last = term(z)
    for j in range(2):
        total = last[j * sub : (j + 1) * sub]
        for d in range(2):
            arrived(run.at[d, j, 0], z_ss.at[d, j, 0], z_rs.at[d, j, 0])
            total += run[d, j, 0].astype(F32)
        for i in range(nt // 2):
            gs[j * (nt // 2) + i] = total[i * rows : (i + 1) * rows].astype(BF16)
    for i in range(1, nt):
        to = lax.rem(t + i, nt)
        send(gs.at[to], gr.at[t], t_ss.at[to], t_rs.at[t], (z, to, b))
    gr[t] = gs[t]

    outs = []

    def weight_part(h):
        both_mem = mem.at[h]
        for k in range(cols // 256):
            lhs = both_mem[:, :, :, :, k * 256 : (k + 1) * 256].reshape(2 * tok, 256)
            for side in range(2):
                core = (c, o)[side]
                rhs = kvs[core].reshape(2 * tok, 256)
                out = lax.dot_general(lhs, rhs, TN, preferred_element_type=F32) * act
                ow[side, h * half + 2 * k] = out[:128].astype(BF16)
                ow[side, h * half + 2 * k + 1] = out[128:].astype(BF16)
        part = pl.ds(h * half, half)
        copy = pltpu.make_async_copy(ow.at[0, part], wg_ref.at[part, c], loc_sem.at[2 + h])
        copy.start()
        outs.append(copy)
        send(ow.at[1, part], wg_ref.at[part, c], o_sem.at[0, h], o_sem.at[1, h], other)

    gather4(0)
    arrived(kvs.at[o, 1 - b], kv_sem.at[4], kv_sem.at[5])
    weight_part(0)

    for i in range(1, nt):
        frm = lax.rem(t + i, nt)
        arrived(gr.at[frm], t_ss.at[frm], t_rs.at[frm])
    sums = [jnp.zeros((rows, 128), F32), jnp.zeros((rows, 128), F32)]
    for i in range(nt):
        sums[i % 2] += gr[i].astype(F32)
    own = jnp.concatenate(sums, axis=1)
    mine = pl.ds(pl.multiple_of(z * 256, 256), 256)
    normed = enc_ref[:, mine] * inv
    scaled = gain_ref[:, mine] * own
    dots = jnp.sum(normed * scaled, axis=1, keepdims=True)
    diagonal = lax.broadcasted_iota(jnp.int32, (rows, 128), 0) == lax.broadcasted_iota(
        jnp.int32, (rows, 128), 1
    )
    hs[...] = jnp.sum(jnp.where(diagonal, dots, 0.0), axis=0, keepdims=True)
    for i in range(1, nz):
        to = lax.rem(z + i, nz)
        send(hs, hr.at[z], h_ss.at[to], h_rs.at[z], (to, t, b))
    hr[z] = hs[...]

    gather4(1)
    weight_part(1)

    for i in range(1, nz):
        frm = lax.rem(z + i, nz)
        arrived(hr.at[frm], h_ss.at[frm], h_rs.at[frm])
    row = jnp.zeros((1, 128), F32)
    for i in range(nz):
        row += hr[i]
    row_dot = jnp.sum(jnp.where(diagonal, row, 0.0), axis=1, keepdims=True) * (1.0 / width)
    eg_ref[...] = (inv * (scaled - normed * row_dot)).astype(BF16)

    for h in range(2):
        part = pl.ds(h * half, half)
        arrived(wg_ref.at[part, o], o_sem.at[0, h], o_sem.at[1, h])
    for copy in outs:
        copy.wait()
    for copy in sent:
        copy.wait_send()


def solution(mesh):
    nz, nt = mesh.shape["section"], mesh.shape["tensor"]

    def per_device(enc_out, gain, weights, kv_grad):
        _, rows, width = enc_out.shape
        tok, hd = kv_grad.shape[2:]
        half = nz // 2
        dma = pltpu.SemaphoreType.DMA
        wg, eg = pl.pallas_call(
            functools.partial(kernel, nz),
            out_shape=(
                jax.ShapeDtypeStruct((nz, 2, 128, hd), BF16),
                jax.ShapeDtypeStruct((rows, 256), BF16),
            ),
            in_specs=[
                pl.BlockSpec(memory_space=pltpu.VMEM),
                pl.BlockSpec(memory_space=pltpu.VMEM),
                pl.BlockSpec(memory_space=pl.ANY),
                pl.BlockSpec(memory_space=pl.ANY),
            ],
            out_specs=(
                pl.BlockSpec(memory_space=pl.ANY),
                pl.BlockSpec(memory_space=pltpu.VMEM),
            ),
            scratch_shapes=[
                pltpu.VMEM((rows, width // 2), BF16),
                pltpu.VMEM((rows, width // 2), BF16),
                pltpu.VMEM((2, 2, X, 2, 2 * rows, half * 128), BF16),
                pltpu.VMEM((2, 2, tok, hd), BF16),
                pltpu.VMEM((2, nz, 128, hd), BF16),
                pltpu.VMEM((2, 2, tok // 2, 128), BF16),
                pltpu.VMEM((2, 2, half, tok // 2, 128), BF16),
                pltpu.VMEM((nt, rows, 128), BF16),
                pltpu.VMEM((nt, rows, 128), BF16),
                pltpu.VMEM((1, 128), F32),
                pltpu.VMEM((nz, 1, 128), F32),
                pltpu.VMEM((2, nz, 128, hd), BF16),
                dma((4,)),
                dma((2,)),
                dma((6,)),
                dma((nz,)),
                dma((nz,)),
                dma((2, 20)),
                dma((2, 20)),
                dma((2, 2, half)),
                dma((2, 2, half)),
                dma((nt,)),
                dma((nt,)),
                dma((nz,)),
                dma((nz,)),
                dma((2, 2)),
            ],
            compiler_params=pltpu.CompilerParams(
                collective_id=0, has_side_effects=True, vmem_limit_bytes=40 * 1024 * 1024
            ),
            cost_estimate=pl.CostEstimate(
                flops=6 * tok * width * hd, bytes_accessed=8 * width * hd, transcendentals=0
            ),
        )(
            enc_out[0],
            gain.reshape(1, width),
            weights.reshape(nz, 2, 128, hd),
            kv_grad[0, 0],
        )
        return wg.reshape(1, width, hd), eg[None]

    return jax.shard_map(
        per_device,
        mesh=mesh,
        in_specs=(
            P("dp", "tensor", None),
            P(),
            P("section", None, "tensor"),
            P("section", "dp", None, "tensor"),
        ),
        out_specs=(P("section", None, "tensor"), P("dp", "tensor", "section")),
        check_vma=False,
    )
```

```python
import functools

import jax
import jax.numpy as jnp
from jax import lax
from jax.experimental import pallas as pl
from jax.experimental.pallas import tpu as pltpu
from jax.sharding import PartitionSpec as P

F32, BF16 = jnp.float32, jnp.bfloat16
X, Y = 4, 4
NT = (((1,), (1,)), ((), ()))
TN = (((0,), (0,)), ((), ()))
PARTS = 4


def kernel(
    nz,
    enc_hbm,
    gain_hbm,
    w_ref,
    kv_ref,
    wg_ref,
    eg_ref,
    enc_ref,
    gain_ref,
    xs,
    xr,
    mem,
    kvs,
    ws,
    tm,
    first,
    run,
    gs,
    gr,
    qa,
    hs,
    hr,
    qs,
    qr,
    ow,
    loc_sem,
    x_sem,
    kv_sem,
    w_ss,
    w_rs,
    ag_ss,
    ag_rs,
    z_ss,
    z_rs,
    t_ss,
    t_rs,
    q_ss,
    q_rs,
    h_ss,
    h_rs,
    o_sem,
):
    z, t, b = lax.axis_index("section"), lax.axis_index("tensor"), lax.axis_index("dp")
    x, yh, c = t // 4, (t // 2) % 2, t % 2
    y = yh * 2 + b
    o = 1 - c
    nt = X * 4
    rows, width = enc_ref.shape
    half = nz // 2
    cols = half * 128
    tok = kvs.shape[2]
    sub = tok // PARTS
    act = (z >= nz // 4).astype(F32)

    def dev(x_, y_, z_, c_):
        return (z_, x_ * 4 + (y_ // 2) * 2 + c_, y_ % 2)

    def remote(src, dst, ss, rs, to):
        return pltpu.make_async_remote_copy(
            src_ref=src,
            dst_ref=dst,
            send_sem=ss,
            recv_sem=rs,
            device_id=to,
            device_id_type=pl.DeviceIdType.MESH,
        )

    other = dev(x, y, z, o)
    sent = []

    def send(src, dst, ss, rs, to):
        copy = remote(src, dst, ss, rs, to)
        copy.start()
        sent.append(copy)

    def arrived(dst, ss, rs):
        remote(dst, dst, ss, rs, other).wait_recv()

    barrier = pltpu.get_barrier_semaphore()

    def greet(to):
        pl.semaphore_signal(barrier, inc=1, device_id=to, device_id_type=pl.DeviceIdType.MESH)

    for i in (8, 7, 9, 6, 10, 5, 11, 4, 12, 3, 13, 2, 14, 1, 15):
        greet((lax.rem(z + i, nz), t, b))
    for i in range(1, nt):
        greet((z, lax.rem(t + i, nt), b))
    greet(dev(x, (y + 1) % Y, z, c))
    greet(dev(x, (y + 3) % Y, z, c))

    enc_load = pltpu.make_async_copy(enc_hbm, enc_ref, loc_sem.at[2])
    enc_load.start()
    gain_load = pltpu.make_async_copy(gain_hbm, gain_ref, loc_sem.at[3])
    gain_load.start()
    kv_load = pltpu.make_async_copy(kv_ref, kvs.at[c, b], loc_sem.at[0])
    kv_load.start()
    w_load = pltpu.make_async_copy(w_ref.at[:, c], ws.at[c], loc_sem.at[1])
    w_load.start()

    enc_load.wait()
    gain_load.wait()
    enc = enc_ref[...]
    inv = lax.rsqrt(jnp.mean(enc * enc, axis=1, keepdims=True) + 1e-06)
    own_cols = []
    for s in range(nz):
        part = (enc[:, s * 256 : (s + 1) * 256] * inv) * gain_ref[:, s * 256 : (s + 1) * 256]
        lo, hi = part[:, :128], part[:, 128:]
        own_cols.append(jnp.where(c == 0, lo, hi))
        xs[:, s * 128 : (s + 1) * 128] = jnp.where(c == 0, hi, lo).astype(BF16)
    kv_load.wait()

    pl.semaphore_wait(barrier, nt - 1 + nz - 1 + 2)

    send(xs, xr, x_sem.at[0], x_sem.at[1], other)
    send(kvs.at[c, b], kvs.at[c, b], kv_sem.at[0], kv_sem.at[1], other)
    order = [half]
    for m in range(half - 1, 0, -1):
        order += [m, nz - m]
    order += [0]
    for m in order:
        d = lax.rem(z + m, nz)
        send(w_ref.at[d, o], ws.at[c, d], w_ss.at[d], w_rs.at[d], other)

    fg = [(x, y), (y, x)]

    def at_xy(h, f, g):
        return (f, g) if h == 0 else (g, f)

    def slot(h, f, g):
        x_, y_ = at_xy(h, f, g)
        return mem.at[h, y_ % 2, x_, y_ // 2]

    def place(h, f, g):
        x_, y_ = at_xy(h, f, g)
        return dev(x_, y_, z, c)

    def along_f(h, off):
        f, g = fg[h]
        s = slot(h, f, g)
        send(s, s, ag_ss.at[h, off - 1], ag_rs.at[h, off - 1], place(h, (f + off) % 4, g))

    def from_f(h, off):
        f, g = fg[h]
        arrived(slot(h, (f + 4 - off) % 4, g), ag_ss.at[h, off - 1], ag_rs.at[h, off - 1])

    def along_g(h, i, off):
        f, g = fg[h]
        s = slot(h, (f + i) % 4, g)
        k = 3 + 3 * i + off - 1
        send(s, s, ag_ss.at[h, k], ag_rs.at[h, k], place(h, f, (g + off) % 4))

    def from_g(h, i, off):
        f, g = fg[h]
        k = 3 + 3 * i + off - 1
        arrived(slot(h, (f + i) % 4, (g + 4 - off) % 4), ag_ss.at[h, k], ag_rs.at[h, k])

    arrived(xr, x_sem.at[0], x_sem.at[1])
    for h in range(2):
        for s in range(half):
            mine = own_cols[h * half + s]
            theirs = xr[:, (h * half + s) * 128 : (h * half + s + 1) * 128].astype(F32)
            both = jnp.concatenate(
                [jnp.where(c == 0, mine, theirs), jnp.where(c == 0, theirs, mine)], axis=0
            )
            mem[h, b, x, yh, :, s * 128 : (s + 1) * 128] = both.astype(BF16)
        if h == 0:
            for off in (1, 3, 2):
                along_f(0, off)
            along_g(0, 0, 2)
    along_f(1, 2)
    for off in (1, 3, 2):
        along_g(1, 0, off)
    for off in (1, 3):
        along_f(1, off)
        along_g(0, 0, off)

    def gather_own():
        for off in (1, 3, 2):
            from_f(0, off)
            along_g(0, (4 - off) % 4, 2)
        from_f(1, 2)
        for off in (1, 3, 2):
            along_g(1, 2, off)

    def gather_rest():
        for off in (1, 3):
            from_f(1, off)
        for i in (1, 3, 2):
            for off in (1, 3):
                along_g(0, i, off)
        for i in (1, 3):
            for off in (1, 3, 2):
                along_g(1, i, off)
        send(kvs.at[c, b], kvs.at[c, b], kv_sem.at[2], kv_sem.at[3], dev(x, yh * 2 + (1 - b), z, c))

    def own_gathered(h):
        if h == 0:
            for i in range(4):
                from_g(0, i, 2)
        else:
            for i in (0, 2):
                for off in (1, 3, 2):
                    from_g(1, i, off)

    def rest_gathered(h):
        if h == 0:
            for i in range(4):
                for off in (1, 3):
                    from_g(0, i, off)
        else:
            for i in (1, 3):
                for off in (1, 3, 2):
                    from_g(1, i, off)

    w_load.wait()
    arrived(kvs.at[o, b], kv_sem.at[0], kv_sem.at[1])

    def term(m):
        d = lax.rem(z + m, nz)
        arrived(ws.at[o, d], w_ss.at[d], w_rs.at[d])
        out = lax.dot_general(kvs[0, b], ws[0, d], NT, preferred_element_type=F32)
        out += lax.dot_general(kvs[1, b], ws[1, d], NT, preferred_element_type=F32)
        tm[d] = out * act

    def hop(k, started):
        for j in range(PARTS):
            for d in range(2):
                start = half if (j < PARTS // 2) == (d == 0) else half - 1
                m = start - k
                if m < 1 or (k == 0 and started != (start == half)):
                    continue
                mine = tm[lax.rem(z + (m, nz - m)[d], nz), j * sub : (j + 1) * sub]
                if k == 0:
                    src = first.at[d, j]
                    src[...] = mine.astype(BF16)
                else:
                    src = run.at[d, j, m]
                    arrived(src, z_ss.at[d, j, m], z_rs.at[d, j, m])
                    src[...] = (src[...].astype(F32) + mine).astype(BF16)
                to = dev(x, y, lax.rem(z + (1, nz - 1)[d], nz), c)
                send(src, run.at[d, j, m - 1], z_ss.at[d, j, m - 1], z_rs.at[d, j, m - 1], to)

    def terms(*ms):
        for m in ms:
            term(m)

    def row_dots():
        for h in range(2):
            own_gathered(h)
        for r in range(X):
            acc = jnp.zeros((sub, 128), F32)
            for s in range(nz):
                at = (s % half) * 128
                m = mem[s // half, b, r, :, :, at : at + 128].reshape(sub, 128)
                acc += tm[s, r * sub : (r + 1) * sub] * m.astype(F32)
            qa[r * sub : (r + 1) * sub] = acc
        total = lax.dot_general(
            jnp.ones((8, 128), F32),
            qa[...],
            NT,
            precision=lax.Precision.HIGHEST,
            preferred_element_type=F32,
        )
        hs[...] = total[:1]
        hr[z] = total[:1]
        for i in (8, 7, 9, 6, 10, 5, 11, 4, 12, 3, 13, 2, 14, 1, 15):
            to = lax.rem(z + i, nz)
            send(hs, hr.at[z], h_ss.at[to], h_rs.at[z], (to, t, b))

    def kv_forward():
        got = kvs.at[c, 1 - b]
        arrived(got, kv_sem.at[2], kv_sem.at[3])
        send(got, got, kv_sem.at[4], kv_sem.at[5], other)

    outs = []

    def weight_pass(h, last):
        rep = 1 - b if last else b
        for k in range(cols // 256):
            lhs = mem[h, rep, :, :, :, k * 256 : (k + 1) * 256].reshape(tok, 256)
            part = pl.ds(h * half + 2 * k, 2)
            for side in (1, 0):
                out = lax.dot_general(
                    lhs, kvs[(c, o)[side], rep], TN, preferred_element_type=F32
                )
                out = (out * act).astype(BF16).reshape(2, 128, out.shape[1])
                if last:
                    out = (ow[side, part].astype(F32) + out.astype(F32)).astype(BF16)
                ow[side, part] = out
                n = h * (cols // 256) + k
                if last and side:
                    send(ow.at[1, part], wg_ref.at[part, c], o_sem.at[0, n], o_sem.at[1, n], other)
                elif last:
                    copy = pltpu.make_async_copy(ow.at[0, part], wg_ref.at[part, c], o_sem.at[2, n])
                    copy.start()
                    outs.append(copy)

    def own_weights():
        for h in range(2):
            weight_pass(h, False)

    def row_dot_sums():
        for i in range(1, nz):
            frm = lax.rem(z + i, nz)
            arrived(hr.at[frm], h_ss.at[frm], h_rs.at[frm])
        total = jnp.zeros((1, tok), F32)
        for i in range(nz):
            total += hr[i]
        qs[...] = total
        qr[t] = total
        for i in range(1, nt):
            to = lax.rem(t + i, nt)
            send(qs, qr.at[t], q_ss.at[to], q_rs.at[t], (z, to, b))

    terms(half)
    hop(0, True)
    terms(half - 1, half + 1)
    hop(0, False)
    inner = list(range(half - 2, 0, -1))
    pairs = [(m, nz - m) for m in inner]
    events = {
        0: [lambda: terms(*pairs[0], *pairs[1])],
        1: [gather_own, lambda: terms(*pairs[2], *pairs[3])],
        2: [gather_rest, lambda: terms(*pairs[4], *pairs[5], 0)],
        4: [row_dots],
        5: [own_weights, kv_forward],
        7: [row_dot_sums],
    }
    for k in range(half):
        if k:
            hop(k, True)
        for event in events.get(k, ()):
            event()

    own = lax.rem(z, nz)
    per = nt // PARTS
    for j in range(PARTS):
        total = tm[own, j * sub : (j + 1) * sub]
        for d in range(2):
            arrived(run.at[d, j, 0], z_ss.at[d, j, 0], z_rs.at[d, j, 0])
            total += run[d, j, 0].astype(F32)
        for i in range(per):
            gs[j * per + i] = total[i * rows : (i + 1) * rows].astype(BF16)
    for i in range(1, nt):
        to = lax.rem(t + i, nt)
        send(gs.at[to], gr.at[t], t_ss.at[to], t_rs.at[t], (z, to, b))
    gr[t] = gs[t]

    arrived(kvs.at[o, 1 - b], kv_sem.at[4], kv_sem.at[5])
    for h in range(2):
        rest_gathered(h)
        weight_pass(h, True)

    for i in range(1, nt):
        frm = lax.rem(t + i, nt)
        arrived(gr.at[frm], t_ss.at[frm], t_rs.at[frm])
        arrived(qr.at[frm], q_ss.at[frm], q_rs.at[frm])
    sums = [jnp.zeros((rows, 128), F32), jnp.zeros((rows, 128), F32)]
    row = jnp.zeros((1, tok), F32)
    for i in range(nt):
        sums[i % 2] += gr[i].astype(F32)
        row += qr[i]
    mine = pl.ds(pl.multiple_of(z * 256, 256), 256)
    normed = enc_ref[:, mine] * inv
    scaled = gain_ref[:, mine] * jnp.concatenate(sums, axis=1)
    token = lax.broadcasted_iota(jnp.int32, (rows, tok), 0) + t * rows
    here = token == lax.broadcasted_iota(jnp.int32, (rows, tok), 1)
    row_dot = jnp.sum(jnp.where(here, row, 0.0), axis=1, keepdims=True) * (1.0 / width)
    eg_ref[...] = (inv * (scaled - normed * row_dot)).astype(BF16)

    for n in range(nz // 2):
        part = pl.ds(2 * n, 2)
        arrived(wg_ref.at[part, o], o_sem.at[0, n], o_sem.at[1, n])
    for copy in outs:
        copy.wait()
    for copy in sent:
        copy.wait_send()


def solution(mesh):
    nz, nt = mesh.shape["section"], mesh.shape["tensor"]

    def per_device(enc_out, gain, weights, kv_grad):
        _, rows, width = enc_out.shape
        tok, hd = kv_grad.shape[2:]
        half = nz // 2
        dma = pltpu.SemaphoreType.DMA
        wg, eg = pl.pallas_call(
            functools.partial(kernel, nz),
            out_shape=(
                jax.ShapeDtypeStruct((nz, 2, 128, hd), BF16),
                jax.ShapeDtypeStruct((rows, 256), BF16),
            ),
            in_specs=[pl.BlockSpec(memory_space=pltpu.HBM)] * 4,
            out_specs=(
                pl.BlockSpec(memory_space=pl.ANY),
                pl.BlockSpec(memory_space=pltpu.VMEM),
            ),
            scratch_shapes=[
                pltpu.VMEM((rows, width), F32),
                pltpu.VMEM((1, width), F32),
                pltpu.VMEM((rows, width // 2), BF16),
                pltpu.VMEM((rows, width // 2), BF16),
                pltpu.VMEM((2, 2, X, 2, 2 * rows, half * 128), BF16),
                pltpu.VMEM((2, 2, tok, hd), BF16),
                pltpu.VMEM((2, nz, 128, hd), BF16),
                pltpu.VMEM((nz, tok, 128), F32),
                pltpu.VMEM((2, PARTS, tok // PARTS, 128), BF16),
                pltpu.VMEM((2, PARTS, half, tok // PARTS, 128), BF16),
                pltpu.VMEM((nt, rows, 128), BF16),
                pltpu.VMEM((nt, rows, 128), BF16),
                pltpu.VMEM((tok, 128), F32),
                pltpu.VMEM((1, tok), F32),
                pltpu.VMEM((nz, 1, tok), F32),
                pltpu.VMEM((1, tok), F32),
                pltpu.VMEM((nt, 1, tok), F32),
                pltpu.VMEM((2, nz, 128, hd), BF16),
                dma((4,)),
                dma((2,)),
                dma((6,)),
                dma((nz,)),
                dma((nz,)),
                dma((2, 15)),
                dma((2, 15)),
                dma((2, PARTS, half)),
                dma((2, PARTS, half)),
                dma((nt,)),
                dma((nt,)),
                dma((nt,)),
                dma((nt,)),
                dma((nz,)),
                dma((nz,)),
                dma((3, nz // 2)),
            ],
            compiler_params=pltpu.CompilerParams(
                collective_id=0, has_side_effects=True, vmem_limit_bytes=32 * 1024 * 1024
            ),
            cost_estimate=pl.CostEstimate(
                flops=6 * tok * width * hd, bytes_accessed=8 * width * hd, transcendentals=0
            ),
        )(
            enc_out[0],
            gain.reshape(1, width),
            weights.reshape(nz, 2, 128, hd),
            kv_grad[0, 0],
        )
        return wg.reshape(1, width, hd), eg[None]

    return jax.shard_map(
        per_device,
        mesh=mesh,
        in_specs=(
            P("dp", "tensor", None),
            P(),
            P("section", None, "tensor"),
            P("section", "dp", None, "tensor"),
        ),
        out_specs=(P("section", None, "tensor"), P("dp", "tensor", "section")),
        check_vma=False,
    )
```

```python
import functools

import jax
import jax.numpy as jnp
from jax import lax
from jax.experimental import pallas as pl
from jax.experimental.pallas import tpu as pltpu
from jax.sharding import PartitionSpec as P

F32, BF16 = jnp.float32, jnp.bfloat16
X, Y = 4, 4
NT = (((1,), (1,)), ((), ()))
TN = (((0,), (0,)), ((), ()))
PARTS = 4


def kernel(
    nz,
    enc_hbm,
    gain_hbm,
    w_ref,
    kv_ref,
    wg_ref,
    eg_ref,
    enc_ref,
    gain_ref,
    xs,
    xr,
    mem,
    kvs,
    ws,
    tm,
    first,
    run,
    gs,
    gr,
    qa,
    hs,
    hr,
    qs,
    qr,
    ow,
    loc_sem,
    x_sem,
    kv_sem,
    w_ss,
    w_rs,
    ag_ss,
    ag_rs,
    z_ss,
    z_rs,
    t_ss,
    t_rs,
    q_ss,
    q_rs,
    h_ss,
    h_rs,
    o_sem,
):
    z, t, b = lax.axis_index("section"), lax.axis_index("tensor"), lax.axis_index("dp")
    x, yh, c = t // 4, (t // 2) % 2, t % 2
    y = yh * 2 + b
    o = 1 - c
    nt = X * 4
    rows, width = enc_ref.shape
    half = nz // 2
    cols = half * 128
    tok = kvs.shape[2]
    sub = tok // PARTS
    act = (z >= nz // 4).astype(F32)

    def dev(x_, y_, z_, c_):
        return (z_, x_ * 4 + (y_ // 2) * 2 + c_, y_ % 2)

    def remote(src, dst, ss, rs, to):
        return pltpu.make_async_remote_copy(
            src_ref=src,
            dst_ref=dst,
            send_sem=ss,
            recv_sem=rs,
            device_id=to,
            device_id_type=pl.DeviceIdType.MESH,
        )

    other = dev(x, y, z, o)
    sent, gathers, marks = [], [], [0]

    def send(src, dst, ss, rs, to, copies=sent):
        copy = remote(src, dst, ss, rs, to)
        copy.start()
        copies.append(copy)

    waited = [0]

    def flush(n):
        for copy in sent[waited[0] : n]:
            copy.wait_send()
        waited[0] = n

    def arrived(dst, ss, rs):
        remote(dst, dst, ss, rs, other).wait_recv()

    barrier = pltpu.get_barrier_semaphore()

    def greet(to):
        pl.semaphore_signal(barrier, inc=1, device_id=to, device_id_type=pl.DeviceIdType.MESH)

    for i in (8, 7, 9, 6, 10, 5, 11, 4, 12, 3, 13, 2, 14, 1, 15):
        greet((lax.rem(z + i, nz), t, b))
    for i in range(1, nt):
        greet((z, lax.rem(t + i, nt), b))
    greet(dev(x, (y + 1) % Y, z, c))
    greet(dev(x, (y + 3) % Y, z, c))

    enc_load = pltpu.make_async_copy(enc_hbm, enc_ref, loc_sem.at[2])
    enc_load.start()
    gain_load = pltpu.make_async_copy(gain_hbm, gain_ref, loc_sem.at[3])
    gain_load.start()
    kv_load = pltpu.make_async_copy(kv_ref, kvs.at[c, b], loc_sem.at[0])
    kv_load.start()
    w_load = pltpu.make_async_copy(w_ref.at[:, c], ws.at[c], loc_sem.at[1])
    w_load.start()

    enc_load.wait()
    gain_load.wait()
    enc = enc_ref[...]
    inv = lax.rsqrt(jnp.mean(enc * enc, axis=1, keepdims=True) + 1e-06)
    own_cols = []
    for s in range(nz):
        part = (enc[:, s * 256 : (s + 1) * 256] * inv) * gain_ref[:, s * 256 : (s + 1) * 256]
        lo, hi = part[:, :128], part[:, 128:]
        own_cols.append(jnp.where(c == 0, lo, hi))
        xs[:, s * 128 : (s + 1) * 128] = jnp.where(c == 0, hi, lo).astype(BF16)
    kv_load.wait()

    pl.semaphore_wait(barrier, nt - 1 + nz - 1 + 2)

    send(xs, xr, x_sem.at[0], x_sem.at[1], other)
    send(kvs.at[c, b], kvs.at[c, b], kv_sem.at[0], kv_sem.at[1], other)
    npair = nz // 2
    order = [npair // 2]
    for r in range(npair // 2 - 1, 0, -1):
        order += [r, npair - r]
    order += [0]

    def pair(r):
        return lax.rem(z // 2 + r, npair)

    for r in order:
        p = pair(r)
        ds = pl.ds(2 * p, 2)
        send(w_ref.at[ds, o], ws.at[c, ds], w_ss.at[p], w_rs.at[p], other)

    fg = [(x, y), (y, x)]

    def at_xy(h, f, g):
        return (f, g) if h == 0 else (g, f)

    def slot(h, f, g):
        x_, y_ = at_xy(h, f, g)
        return mem.at[h, y_ % 2, x_, y_ // 2]

    def place(h, f, g):
        x_, y_ = at_xy(h, f, g)
        return dev(x_, y_, z, c)

    def along_f(h, off):
        f, g = fg[h]
        s = slot(h, f, g)
        to = place(h, (f + off) % 4, g)
        send(s, s, ag_ss.at[h, off - 1], ag_rs.at[h, off - 1], to, gathers)

    def from_f(h, off):
        f, g = fg[h]
        arrived(slot(h, (f + 4 - off) % 4, g), ag_ss.at[h, off - 1], ag_rs.at[h, off - 1])

    def along_g(h, i, off):
        f, g = fg[h]
        s = slot(h, (f + i) % 4, g)
        k = 3 + 3 * i + off - 1
        send(s, s, ag_ss.at[h, k], ag_rs.at[h, k], place(h, f, (g + off) % 4), gathers)

    def from_g(h, i, off):
        f, g = fg[h]
        k = 3 + 3 * i + off - 1
        arrived(slot(h, (f + i) % 4, (g + 4 - off) % 4), ag_ss.at[h, k], ag_rs.at[h, k])

    arrived(xr, x_sem.at[0], x_sem.at[1])
    for h in range(2):
        for s in range(half):
            mine = own_cols[h * half + s]
            theirs = xr[:, (h * half + s) * 128 : (h * half + s + 1) * 128].astype(F32)
            both = jnp.concatenate(
                [jnp.where(c == 0, mine, theirs), jnp.where(c == 0, theirs, mine)], axis=0
            )
            mem[h, b, x, yh, :, s * 128 : (s + 1) * 128] = both.astype(BF16)
        if h == 0:
            for off in (1, 3, 2):
                along_f(0, off)
    along_f(1, 2)

    def gather_start():
        along_g(0, 0, 2)
        for off in (1, 3, 2):
            along_g(1, 0, off)
        for off in (1, 3):
            along_f(1, off)
            along_g(0, 0, off)

    def gather_own():
        for off in (1, 3, 2):
            from_f(0, off)
            along_g(0, (4 - off) % 4, 2)
        from_f(1, 2)
        for off in (1, 3, 2):
            along_g(1, 2, off)

    def gather_rest():
        for off in (1, 3):
            from_f(1, off)
        for i in (1, 3, 2):
            for off in (1, 3):
                along_g(0, i, off)
        for i in (1, 3):
            for off in (1, 3, 2):
                along_g(1, i, off)
        mine = kvs.at[c, b]
        send(mine, mine, kv_sem.at[2], kv_sem.at[3], dev(x, yh * 2 + (1 - b), z, c), gathers)

    def own_gathered(h):
        if h == 0:
            for i in range(4):
                from_g(0, i, 2)
        else:
            for i in (0, 2):
                for off in (1, 3, 2):
                    from_g(1, i, off)

    def rest_gathered(h):
        if h == 0:
            for i in range(4):
                for off in (1, 3):
                    from_g(0, i, off)
        else:
            for i in (1, 3):
                for off in (1, 3, 2):
                    from_g(1, i, off)

    w_load.wait()
    arrived(kvs.at[o, b], kv_sem.at[0], kv_sem.at[1])

    def term(r):
        p = pair(r)
        ds = pl.ds(2 * p, 2)
        arrived(ws.at[o, ds], w_ss.at[p], w_rs.at[p])
        out = jnp.zeros((tok, 256), F32)
        for core in range(2):
            rhs = ws[core, ds].reshape(256, ws.shape[3])
            out += lax.dot_general(kvs[core, b], rhs, NT, preferred_element_type=F32)
        out *= act
        tm[2 * p] = out[:, :128]
        tm[2 * p + 1] = out[:, 128:]

    def hop(k, started):
        for j in range(PARTS):
            for d in range(2):
                start = half if (j < PARTS // 2) == (d == 0) else half - 1
                m = start - k
                if m < 1 or (k == 0 and started != (start == half)):
                    continue
                mine = tm[lax.rem(z + (m, nz - m)[d], nz), j * sub : (j + 1) * sub]
                if k == 0:
                    src = first.at[d, j]
                    src[...] = mine.astype(BF16)
                else:
                    src = run.at[d, j, m]
                    arrived(src, z_ss.at[d, j, m], z_rs.at[d, j, m])
                    src[...] = (src[...].astype(F32) + mine).astype(BF16)
                to = dev(x, y, lax.rem(z + (1, nz - 1)[d], nz), c)
                send(src, run.at[d, j, m - 1], z_ss.at[d, j, m - 1], z_rs.at[d, j, m - 1], to)

    def terms(*rs):
        for r in rs:
            term(r)

    def row_dots():
        for h in range(2):
            own_gathered(h)
        for r in range(X):
            acc = jnp.zeros((sub, 128), F32)
            for s in range(nz):
                at = (s % half) * 128
                m = mem[s // half, b, r, :, :, at : at + 128].reshape(sub, 128)
                acc += tm[s, r * sub : (r + 1) * sub] * m.astype(F32)
            qa[r * sub : (r + 1) * sub] = acc
        total = lax.dot_general(
            jnp.ones((8, 128), F32),
            qa[...],
            NT,
            precision=lax.Precision.HIGHEST,
            preferred_element_type=F32,
        )
        hs[...] = total[:1]
        hr[z] = total[:1]
        for i in (8, 7, 9, 6, 10, 5, 11, 4, 12, 3, 13, 2, 14, 1, 15):
            to = lax.rem(z + i, nz)
            send(hs, hr.at[z], h_ss.at[to], h_rs.at[z], (to, t, b))

    def kv_forward():
        got = kvs.at[c, 1 - b]
        arrived(got, kv_sem.at[2], kv_sem.at[3])
        send(got, got, kv_sem.at[4], kv_sem.at[5], other)

    outs = []

    def weight_pass(h, last):
        rep = 1 - b if last else b
        for k in range(cols // 256):
            lhs = mem[h, rep, :, :, :, k * 256 : (k + 1) * 256].reshape(tok, 256)
            part = pl.ds(h * half + 2 * k, 2)
            for side in (1, 0):
                out = lax.dot_general(
                    lhs, kvs[(c, o)[side], rep], TN, preferred_element_type=F32
                )
                out = (out * act).astype(BF16).reshape(2, 128, out.shape[1])
                if last:
                    out = (ow[side, part].astype(F32) + out.astype(F32)).astype(BF16)
                ow[side, part] = out
                n = h * (cols // 256) + k
                if last and side:
                    send(ow.at[1, part], wg_ref.at[part, c], o_sem.at[0, n], o_sem.at[1, n], other)
                elif last:
                    copy = pltpu.make_async_copy(ow.at[0, part], wg_ref.at[part, c], o_sem.at[2, n])
                    copy.start()
                    outs.append(copy)

    def own_weights():
        for h in range(2):
            weight_pass(h, False)

    def row_dot_sums():
        for i in range(1, nz):
            frm = lax.rem(z + i, nz)
            arrived(hr.at[frm], h_ss.at[frm], h_rs.at[frm])
        total = jnp.zeros((1, tok), F32)
        for i in range(nz):
            total += hr[i]
        qs[...] = total
        qr[t] = total
        for i in range(1, nt):
            to = lax.rem(t + i, nt)
            send(qs, qr.at[t], q_ss.at[to], q_rs.at[t], (z, to, b))

    term(order[0])
    hop(0, True)
    gather_start()
    terms(*order[1:3])
    hop(0, False)
    events = {
        0: [lambda: terms(*order[3:5])],
        1: [gather_own, lambda: terms(*order[5:7])],
        2: [gather_rest, lambda: terms(order[7])],
        5: [row_dots],
        6: [own_weights, kv_forward],
        7: [row_dot_sums],
    }
    for k in range(half):
        if k:
            hop(k, True)
        for event in events.get(k, ()):
            event()
        if k >= 2:
            flush(marks[k - 1])
        marks.append(len(sent))

    own = lax.rem(z, nz)
    per = nt // PARTS
    for j in range(PARTS):
        total = tm[own, j * sub : (j + 1) * sub]
        for d in range(2):
            arrived(run.at[d, j, 0], z_ss.at[d, j, 0], z_rs.at[d, j, 0])
            total += run[d, j, 0].astype(F32)
        for i in range(per):
            gs[j * per + i] = total[i * rows : (i + 1) * rows].astype(BF16)
    before_last = len(sent)
    for i in range(1, nt):
        to = lax.rem(t + i, nt)
        send(gs.at[to], gr.at[t], t_ss.at[to], t_rs.at[t], (z, to, b))
    gr[t] = gs[t]

    arrived(kvs.at[o, 1 - b], kv_sem.at[4], kv_sem.at[5])
    for h in range(2):
        rest_gathered(h)
        weight_pass(h, True)

    for copy in gathers:
        copy.wait_send()
    flush(before_last)

    for i in range(1, nt):
        frm = lax.rem(t + i, nt)
        arrived(gr.at[frm], t_ss.at[frm], t_rs.at[frm])
        arrived(qr.at[frm], q_ss.at[frm], q_rs.at[frm])
    sums = [jnp.zeros((rows, 128), F32), jnp.zeros((rows, 128), F32)]
    row = jnp.zeros((1, tok), F32)
    for i in range(nt):
        sums[i % 2] += gr[i].astype(F32)
        row += qr[i]
    mine = pl.ds(pl.multiple_of(z * 256, 256), 256)
    normed = enc_ref[:, mine] * inv
    scaled = gain_ref[:, mine] * jnp.concatenate(sums, axis=1)
    token = lax.broadcasted_iota(jnp.int32, (rows, tok), 0) + t * rows
    here = token == lax.broadcasted_iota(jnp.int32, (rows, tok), 1)
    row_dot = jnp.sum(jnp.where(here, row, 0.0), axis=1, keepdims=True) * (1.0 / width)
    eg_ref[...] = (inv * (scaled - normed * row_dot)).astype(BF16)

    for n in range(nz // 2):
        part = pl.ds(2 * n, 2)
        arrived(wg_ref.at[part, o], o_sem.at[0, n], o_sem.at[1, n])
    for copy in outs:
        copy.wait()
    flush(len(sent))


def solution(mesh):
    nz, nt = mesh.shape["section"], mesh.shape["tensor"]

    def per_device(enc_out, gain, weights, kv_grad):
        _, rows, width = enc_out.shape
        tok, hd = kv_grad.shape[2:]
        half = nz // 2
        dma = pltpu.SemaphoreType.DMA
        wg, eg = pl.pallas_call(
            functools.partial(kernel, nz),
            out_shape=(
                jax.ShapeDtypeStruct((nz, 2, 128, hd), BF16),
                jax.ShapeDtypeStruct((rows, 256), BF16),
            ),
            in_specs=[pl.BlockSpec(memory_space=pltpu.HBM)] * 4,
            out_specs=(
                pl.BlockSpec(memory_space=pl.ANY),
                pl.BlockSpec(memory_space=pltpu.VMEM),
            ),
            scratch_shapes=[
                pltpu.VMEM((rows, width), F32),
                pltpu.VMEM((1, width), F32),
                pltpu.VMEM((rows, width // 2), BF16),
                pltpu.VMEM((rows, width // 2), BF16),
                pltpu.VMEM((2, 2, X, 2, 2 * rows, half * 128), BF16),
                pltpu.VMEM((2, 2, tok, hd), BF16),
                pltpu.VMEM((2, nz, 128, hd), BF16),
                pltpu.VMEM((nz, tok, 128), F32),
                pltpu.VMEM((2, PARTS, tok // PARTS, 128), BF16),
                pltpu.VMEM((2, PARTS, half, tok // PARTS, 128), BF16),
                pltpu.VMEM((nt, rows, 128), BF16),
                pltpu.VMEM((nt, rows, 128), BF16),
                pltpu.VMEM((tok, 128), F32),
                pltpu.VMEM((1, tok), F32),
                pltpu.VMEM((nz, 1, tok), F32),
                pltpu.VMEM((1, tok), F32),
                pltpu.VMEM((nt, 1, tok), F32),
                pltpu.VMEM((2, nz, 128, hd), BF16),
                dma((4,)),
                dma((2,)),
                dma((6,)),
                dma((nz // 2,)),
                dma((nz // 2,)),
                dma((2, 15)),
                dma((2, 15)),
                dma((2, PARTS, half)),
                dma((2, PARTS, half)),
                dma((nt,)),
                dma((nt,)),
                dma((nt,)),
                dma((nt,)),
                dma((nz,)),
                dma((nz,)),
                dma((3, nz // 2)),
            ],
            compiler_params=pltpu.CompilerParams(
                collective_id=0, has_side_effects=True, vmem_limit_bytes=32 * 1024 * 1024
            ),
            cost_estimate=pl.CostEstimate(
                flops=6 * tok * width * hd, bytes_accessed=8 * width * hd, transcendentals=0
            ),
        )(
            *(
                pltpu.with_memory_space_constraint(a, pltpu.HBM)
                for a in (
                    enc_out[0],
                    gain.reshape(1, width),
                    weights.reshape(nz, 2, 128, hd),
                    kv_grad[0, 0],
                )
            )
        )
        return wg.reshape(1, width, hd), eg[None]

    return jax.shard_map(
        per_device,
        mesh=mesh,
        in_specs=(
            P("dp", "tensor", None),
            P(),
            P("section", None, "tensor"),
            P("section", "dp", None, "tensor"),
        ),
        out_specs=(P("section", None, "tensor"), P("dp", "tensor", "section")),
        check_vma=False,
    )
```

```python
import functools

import jax
import jax.numpy as jnp
from jax import lax
from jax.experimental import pallas as pl
from jax.experimental.pallas import tpu as pltpu
from jax.sharding import PartitionSpec as P

F32, BF16 = jnp.float32, jnp.bfloat16
X, Y = 4, 4
NT = (((1,), (1,)), ((), ()))
TN = (((0,), (0,)), ((), ()))
PARTS = 4


def kernel(
    nz,
    enc_hbm,
    gain_hbm,
    w_ref,
    kv_ref,
    wg_ref,
    eg_ref,
    enc_ref,
    gain_ref,
    xs,
    xr,
    mem,
    kvs,
    ws,
    tm,
    first,
    run,
    gs,
    gr,
    qa,
    hs,
    hr,
    qs,
    qr,
    ow,
    loc_sem,
    x_sem,
    kv_sem,
    w_ss,
    w_rs,
    ag_ss,
    ag_rs,
    z_ss,
    z_rs,
    t_ss,
    t_rs,
    q_ss,
    q_rs,
    h_ss,
    h_rs,
    o_sem,
    hello,
):
    z, t, b = lax.axis_index("section"), lax.axis_index("tensor"), lax.axis_index("dp")
    x, yh, c = t // 4, (t // 2) % 2, t % 2
    y = yh * 2 + b
    o = 1 - c
    nt = X * 4
    rows, width = enc_ref.shape
    half = nz // 2
    cols = half * 128
    tok = kvs.shape[2]
    sub = tok // PARTS
    act = (z >= nz // 4).astype(F32)

    def dev(x_, y_, z_, c_):
        return (z_, x_ * 4 + (y_ // 2) * 2 + c_, y_ % 2)

    def remote(src, dst, ss, rs, to):
        return pltpu.make_async_remote_copy(
            src_ref=src,
            dst_ref=dst,
            send_sem=ss,
            recv_sem=rs,
            device_id=to,
            device_id_type=pl.DeviceIdType.MESH,
        )

    other = dev(x, y, z, o)
    sent, gathers, marks = [], [], [0]

    def send(src, dst, ss, rs, to, copies=sent):
        copy = remote(src, dst, ss, rs, to)
        copy.start()
        copies.append(copy)

    waited = [0]

    def flush(n):
        for copy in sent[waited[0] : n]:
            copy.wait_send()
        waited[0] = n

    def arrived(dst, ss, rs):
        remote(dst, dst, ss, rs, other).wait_recv()

    enc_load = pltpu.make_async_copy(enc_hbm, enc_ref, loc_sem.at[2])
    enc_load.start()
    gain_load = pltpu.make_async_copy(gain_hbm, gain_ref, loc_sem.at[3])
    gain_load.start()
    kv_load = pltpu.make_async_copy(kv_ref, kvs.at[c, b], loc_sem.at[0])
    kv_load.start()
    w_load = pltpu.make_async_copy(w_ref.at[:, c], ws.at[c], loc_sem.at[1])
    w_load.start()

    barrier = pltpu.get_barrier_semaphore()

    def greet(to):
        pl.semaphore_signal(barrier, inc=1, device_id=to, device_id_type=pl.DeviceIdType.MESH)

    greet(other)
    far = half // 2
    for i in (1, nz - 1, far, nz - far):
        greet((lax.rem(z + i, nz), t, b))
    for i in range(1, X):
        greet(dev((x + i) % X, y, z, c))
    for i in range(1, Y):
        greet(dev(x, (y + i) % Y, z, c))

    enc_load.wait()
    gain_load.wait()
    enc = enc_ref[...]
    inv = lax.rsqrt(jnp.mean(enc * enc, axis=1, keepdims=True) + 1e-06)
    own_cols = []
    for s in range(nz):
        part = (enc[:, s * 256 : (s + 1) * 256] * inv) * gain_ref[:, s * 256 : (s + 1) * 256]
        lo, hi = part[:, :128], part[:, 128:]
        own_cols.append(jnp.where(c == 0, lo, hi))
        xs[:, s * 128 : (s + 1) * 128] = jnp.where(c == 0, hi, lo).astype(BF16)
    kv_load.wait()

    pl.semaphore_wait(barrier, 1 + 4 + X - 1 + Y - 1)

    send(xs, xr, x_sem.at[0], x_sem.at[1], other)
    send(kvs.at[c, b], kvs.at[c, b], kv_sem.at[0], kv_sem.at[1], other)
    npair = nz // 2
    order = [npair // 2]
    for r in range(npair // 2 - 1, 0, -1):
        order += [r, npair - r]
    order += [0]

    def pair(r):
        return lax.rem(z // 2 + r, npair)

    for r in order:
        p = pair(r)
        ds = pl.ds(2 * p, 2)
        send(w_ref.at[ds, o], ws.at[c, ds], w_ss.at[p], w_rs.at[p], other)

    fg = [(x, y), (y, x)]

    def at_xy(h, f, g):
        return (f, g) if h == 0 else (g, f)

    def slot(h, f, g):
        x_, y_ = at_xy(h, f, g)
        return mem.at[h, y_ % 2, x_, y_ // 2]

    def place(h, f, g):
        x_, y_ = at_xy(h, f, g)
        return dev(x_, y_, z, c)

    def along_f(h, off):
        f, g = fg[h]
        s = slot(h, f, g)
        to = place(h, (f + off) % 4, g)
        send(s, s, ag_ss.at[h, off - 1], ag_rs.at[h, off - 1], to, gathers)

    def from_f(h, off):
        f, g = fg[h]
        arrived(slot(h, (f + 4 - off) % 4, g), ag_ss.at[h, off - 1], ag_rs.at[h, off - 1])

    def along_g(h, i, off):
        f, g = fg[h]
        s = slot(h, (f + i) % 4, g)
        k = 3 + 3 * i + off - 1
        send(s, s, ag_ss.at[h, k], ag_rs.at[h, k], place(h, f, (g + off) % 4), gathers)

    def from_g(h, i, off):
        f, g = fg[h]
        k = 3 + 3 * i + off - 1
        arrived(slot(h, (f + i) % 4, (g + 4 - off) % 4), ag_ss.at[h, k], ag_rs.at[h, k])

    arrived(xr, x_sem.at[0], x_sem.at[1])
    for h in range(2):
        for s in range(half):
            mine = own_cols[h * half + s]
            theirs = xr[:, (h * half + s) * 128 : (h * half + s + 1) * 128].astype(F32)
            both = jnp.concatenate(
                [jnp.where(c == 0, mine, theirs), jnp.where(c == 0, theirs, mine)], axis=0
            )
            mem[h, b, x, yh, :, s * 128 : (s + 1) * 128] = both.astype(BF16)
        if h == 0:
            for off in (1, 3, 2):
                along_f(0, off)
    along_f(1, 2)

    def gather_start():
        along_g(0, 0, 2)
        for off in (1, 3, 2):
            along_g(1, 0, off)
        for off in (1, 3):
            along_f(1, off)
            along_g(0, 0, off)

    def gather_own():
        for off in (1, 3, 2):
            from_f(0, off)
            along_g(0, (4 - off) % 4, 2)
        from_f(1, 2)
        for off in (1, 3, 2):
            along_g(1, 2, off)

    def gather_rest():
        for off in (1, 3):
            from_f(1, off)
        for i in (1, 3, 2):
            for off in (1, 3):
                along_g(0, i, off)
        for i in (1, 3):
            for off in (1, 3, 2):
                along_g(1, i, off)
        mine = kvs.at[c, b]
        send(mine, mine, kv_sem.at[2], kv_sem.at[3], dev(x, yh * 2 + (1 - b), z, c), gathers)

    def own_gathered(h):
        if h == 0:
            for i in range(4):
                from_g(0, i, 2)
        else:
            for i in (0, 2):
                for off in (1, 3, 2):
                    from_g(1, i, off)

    def rest_gathered(h):
        if h == 0:
            for i in range(4):
                for off in (1, 3):
                    from_g(0, i, off)
        else:
            for i in (1, 3):
                for off in (1, 3, 2):
                    from_g(1, i, off)

    w_load.wait()
    arrived(kvs.at[o, b], kv_sem.at[0], kv_sem.at[1])

    def term(r):
        p = pair(r)
        ds = pl.ds(2 * p, 2)
        arrived(ws.at[o, ds], w_ss.at[p], w_rs.at[p])
        out = jnp.zeros((tok, 256), F32)
        for core in range(2):
            rhs = ws[core, ds].reshape(256, ws.shape[3])
            out += lax.dot_general(kvs[core, b], rhs, NT, preferred_element_type=F32)
        out *= act
        tm[2 * p] = out[:, :128]
        tm[2 * p + 1] = out[:, 128:]

    def hop(k, started):
        for j in range(PARTS):
            for d in range(2):
                start = half if (j < PARTS // 2) == (d == 0) else half - 1
                m = start - k
                if m < 1 or (k == 0 and started != (start == half)):
                    continue
                mine = tm[lax.rem(z + (m, nz - m)[d], nz), j * sub : (j + 1) * sub]
                if k == 0:
                    src = first.at[d, j]
                    src[...] = mine.astype(BF16)
                else:
                    src = run.at[d, j, m]
                    arrived(src, z_ss.at[d, j, m], z_rs.at[d, j, m])
                    src[...] = (src[...].astype(F32) + mine).astype(BF16)
                to = dev(x, y, lax.rem(z + (1, nz - 1)[d], nz), c)
                send(src, run.at[d, j, m - 1], z_ss.at[d, j, m - 1], z_rs.at[d, j, m - 1], to)

    def terms(*rs):
        for r in rs:
            term(r)

    def say_hello():
        for i in (far, nz - far):
            to = (lax.rem(z + i, nz), t, b)
            pl.semaphore_signal(hello, inc=1, device_id=to, device_id_type=pl.DeviceIdType.MESH)

    def row_dots():
        for h in range(2):
            own_gathered(h)
        blk = tok // X
        for r in range(X):
            acc = jnp.zeros((blk, 128), F32)
            for s in range(nz):
                at = (s % half) * 128
                m = mem[s // half, b, r, :, :, at : at + 128].reshape(blk, 128)
                acc += tm[s, r * blk : (r + 1) * blk] * m.astype(F32)
            qa[r * blk : (r + 1) * blk] = acc
        total = lax.dot_general(
            jnp.ones((8, 128), F32),
            qa[...],
            NT,
            precision=lax.Precision.HIGHEST,
            preferred_element_type=F32,
        )
        hs[...] = total[:1]
        hr[z] = total[:1]
        pl.semaphore_wait(hello, 2)
        for i in (8, 7, 9, 6, 10, 5, 11, 4, 12, 3, 13, 2, 14, 1, 15):
            to = lax.rem(z + i, nz)
            send(hs, hr.at[z], h_ss.at[to], h_rs.at[z], (to, t, b))

    def kv_forward():
        got = kvs.at[c, 1 - b]
        arrived(got, kv_sem.at[2], kv_sem.at[3])
        send(got, got, kv_sem.at[4], kv_sem.at[5], other)

    outs = []

    def weight_pass(h, last):
        rep = 1 - b if last else b
        for k in range(cols // 256):
            lhs = mem[h, rep, :, :, :, k * 256 : (k + 1) * 256].reshape(tok, 256)
            part = pl.ds(h * half + 2 * k, 2)
            for side in (1, 0):
                out = lax.dot_general(
                    lhs, kvs[(c, o)[side], rep], TN, preferred_element_type=F32
                )
                out = (out * act).astype(BF16).reshape(2, 128, out.shape[1])
                if last:
                    out = (ow[side, part].astype(F32) + out.astype(F32)).astype(BF16)
                ow[side, part] = out
                n = h * (cols // 256) + k
                if last and side:
                    send(ow.at[1, part], wg_ref.at[part, c], o_sem.at[0, n], o_sem.at[1, n], other)
                elif last:
                    copy = pltpu.make_async_copy(ow.at[0, part], wg_ref.at[part, c], o_sem.at[2, n])
                    copy.start()
                    outs.append(copy)

    def own_weights():
        for h in range(2):
            weight_pass(h, False)

    def row_dot_sums():
        for i in range(1, nz):
            frm = lax.rem(z + i, nz)
            arrived(hr.at[frm], h_ss.at[frm], h_rs.at[frm])
        total = jnp.zeros((1, tok), F32)
        for i in range(nz):
            total += hr[i]
        qs[...] = total
        qr[t] = total
        for i in range(1, nt):
            to = lax.rem(t + i, nt)
            send(qs, qr.at[t], q_ss.at[to], q_rs.at[t], (z, to, b))

    term(order[0])
    hop(0, True)
    gather_start()
    terms(*order[1:3])
    hop(0, False)
    events = {
        0: [lambda: terms(*order[3:5])],
        1: [gather_own, lambda: terms(*order[5:7])],
        2: [gather_rest, lambda: terms(order[7])],
        4: [say_hello],
        5: [row_dots],
        6: [own_weights, kv_forward],
        7: [row_dot_sums],
    }
    for k in range(half):
        if k:
            hop(k, True)
        for event in events.get(k, ()):
            event()
        if k >= 2:
            flush(marks[k - 1])
        marks.append(len(sent))

    per = nt // PARTS

    def piece(i):
        return remote(gs.at[i], gr.at[t], t_ss.at[i], t_rs.at[t], (z, i, b))

    for j in range(PARTS):
        total = tm[z, j * sub : (j + 1) * sub]
        for d in range(2):
            arrived(run.at[d, j, 0], z_ss.at[d, j, 0], z_rs.at[d, j, 0])
            total += run[d, j, 0].astype(F32)
        for i in range(j * per, (j + 1) * per):
            r = (i - j * per) * rows
            gs[i] = total[r : r + rows].astype(BF16)
        for i in range(j * per, (j + 1) * per):
            pl.when(i != t)(piece(i).start)
    gr[t] = gs[t]
    arrived(kvs.at[o, 1 - b], kv_sem.at[4], kv_sem.at[5])
    for h in range(2):
        rest_gathered(h)
        weight_pass(h, True)

    for copy in gathers:
        copy.wait_send()
    flush(len(sent) - nz // 2)

    for i in range(1, nt):
        frm = lax.rem(t + i, nt)
        arrived(qr.at[frm], q_ss.at[frm], q_rs.at[frm])
    row = jnp.zeros((1, tok), F32)
    for i in range(nt):
        row += qr[i]
    mine = pl.ds(pl.multiple_of(z * 256, 256), 256)
    normed = enc_ref[:, mine] * inv
    token = lax.broadcasted_iota(jnp.int32, (rows, tok), 0) + t * rows
    here = token == lax.broadcasted_iota(jnp.int32, (rows, tok), 1)
    row_dot = jnp.sum(jnp.where(here, row, 0.0), axis=1, keepdims=True) * (1.0 / width)
    for i in range(1, nt):
        frm = lax.rem(t + i, nt)
        arrived(gr.at[frm], t_ss.at[frm], t_rs.at[frm])
    sums = [jnp.zeros((rows, 128), F32), jnp.zeros((rows, 128), F32)]
    for i in range(nt):
        sums[i % 2] += gr[i].astype(F32)
    scaled = gain_ref[:, mine] * jnp.concatenate(sums, axis=1)
    eg_ref[...] = (inv * (scaled - normed * row_dot)).astype(BF16)

    for n in range(nz // 2):
        part = pl.ds(2 * n, 2)
        arrived(wg_ref.at[part, o], o_sem.at[0, n], o_sem.at[1, n])
    for copy in outs:
        copy.wait()
    flush(len(sent))
    for i in range(nt):
        pl.when(i != t)(piece(i).wait_send)


def solution(mesh):
    nz, nt = mesh.shape["section"], mesh.shape["tensor"]

    def per_device(enc_out, gain, weights, kv_grad):
        _, rows, width = enc_out.shape
        tok, hd = kv_grad.shape[2:]
        half = nz // 2
        dma = pltpu.SemaphoreType.DMA
        wg, eg = pl.pallas_call(
            functools.partial(kernel, nz),
            out_shape=(
                jax.ShapeDtypeStruct((nz, 2, 128, hd), BF16),
                jax.ShapeDtypeStruct((rows, 256), BF16),
            ),
            in_specs=[pl.BlockSpec(memory_space=pltpu.HBM)] * 4,
            out_specs=(
                pl.BlockSpec(memory_space=pl.ANY),
                pl.BlockSpec(memory_space=pltpu.VMEM),
            ),
            scratch_shapes=[
                pltpu.VMEM((rows, width), F32),
                pltpu.VMEM((1, width), F32),
                pltpu.VMEM((rows, width // 2), BF16),
                pltpu.VMEM((rows, width // 2), BF16),
                pltpu.VMEM((2, 2, X, 2, 2 * rows, half * 128), BF16),
                pltpu.VMEM((2, 2, tok, hd), BF16),
                pltpu.VMEM((2, nz, 128, hd), BF16),
                pltpu.VMEM((nz, tok, 128), F32),
                pltpu.VMEM((2, PARTS, tok // PARTS, 128), BF16),
                pltpu.VMEM((2, PARTS, half, tok // PARTS, 128), BF16),
                pltpu.VMEM((nt, rows, 128), BF16),
                pltpu.VMEM((nt, rows, 128), BF16),
                pltpu.VMEM((tok, 128), F32),
                pltpu.VMEM((1, tok), F32),
                pltpu.VMEM((nz, 1, tok), F32),
                pltpu.VMEM((1, tok), F32),
                pltpu.VMEM((nt, 1, tok), F32),
                pltpu.VMEM((2, nz, 128, hd), BF16),
                dma((4,)),
                dma((2,)),
                dma((6,)),
                dma((nz // 2,)),
                dma((nz // 2,)),
                dma((2, 15)),
                dma((2, 15)),
                dma((2, PARTS, half)),
                dma((2, PARTS, half)),
                dma((nt,)),
                dma((nt,)),
                dma((nt,)),
                dma((nt,)),
                dma((nz,)),
                dma((nz,)),
                dma((3, nz // 2)),
                pltpu.SemaphoreType.REGULAR,
            ],
            compiler_params=pltpu.CompilerParams(
                collective_id=0, has_side_effects=True, vmem_limit_bytes=32 * 1024 * 1024
            ),
            cost_estimate=pl.CostEstimate(
                flops=6 * tok * width * hd, bytes_accessed=8 * width * hd, transcendentals=0
            ),
        )(
            *(
                pltpu.with_memory_space_constraint(a, pltpu.HBM)
                for a in (
                    enc_out[0],
                    gain.reshape(1, width),
                    weights.reshape(nz, 2, 128, hd),
                    kv_grad[0, 0],
                )
            )
        )
        return wg.reshape(1, width, hd), eg[None]

    return jax.shard_map(
        per_device,
        mesh=mesh,
        in_specs=(
            P("dp", "tensor", None),
            P(),
            P("section", None, "tensor"),
            P("section", "dp", None, "tensor"),
        ),
        out_specs=(P("section", None, "tensor"), P("dp", "tensor", "section")),
        check_vma=False,
    )
```

```python
import functools

import jax
import jax.numpy as jnp
from jax import lax
from jax.experimental import pallas as pl
from jax.experimental.pallas import tpu as pltpu
from jax.sharding import PartitionSpec as P

F32, BF16 = jnp.float32, jnp.bfloat16
X, Y = 4, 4
NT = (((1,), (1,)), ((), ()))
TN = (((0,), (0,)), ((), ()))
PARTS = 4


def kernel(
    nz,
    enc_hbm,
    gain_hbm,
    w_ref,
    kv_ref,
    wg_ref,
    eg_ref,
    enc_ref,
    gain_ref,
    xs,
    xr,
    mem,
    kvs,
    ws,
    tm,
    first,
    run,
    gs,
    gr,
    qa,
    hs,
    hr,
    qs,
    qr,
    ow,
    loc_sem,
    x_sem,
    kv_sem,
    w_ss,
    w_rs,
    ag_ss,
    ag_rs,
    z_ss,
    z_rs,
    t_ss,
    t_rs,
    q_ss,
    q_rs,
    h_ss,
    h_rs,
    o_sem,
    hello,
):
    z, t, b = lax.axis_index("section"), lax.axis_index("tensor"), lax.axis_index("dp")
    x, yh, c = t // 4, (t // 2) % 2, t % 2
    y = yh * 2 + b
    o = 1 - c
    nt = X * 4
    rows, width = enc_ref.shape
    half = nz // 2
    cols = half * 128
    tok = kvs.shape[2]
    sub = tok // PARTS
    act = (z >= nz // 4).astype(F32)

    def dev(x_, y_, z_, c_):
        return (z_, x_ * 4 + (y_ // 2) * 2 + c_, y_ % 2)

    def remote(src, dst, ss, rs, to):
        return pltpu.make_async_remote_copy(
            src_ref=src,
            dst_ref=dst,
            send_sem=ss,
            recv_sem=rs,
            device_id=to,
            device_id_type=pl.DeviceIdType.MESH,
        )

    other = dev(x, y, z, o)
    sent, gathers, marks = [], [], [0]

    def send(src, dst, ss, rs, to, copies=sent):
        copy = remote(src, dst, ss, rs, to)
        copy.start()
        copies.append(copy)

    waited = [0]

    def flush(n):
        for copy in sent[waited[0] : n]:
            copy.wait_send()
        waited[0] = n

    def arrived(dst, ss, rs):
        remote(dst, dst, ss, rs, other).wait_recv()

    enc_load = pltpu.make_async_copy(enc_hbm, enc_ref, loc_sem.at[2])
    enc_load.start()
    gain_load = pltpu.make_async_copy(gain_hbm, gain_ref, loc_sem.at[3])
    gain_load.start()
    kv_load = pltpu.make_async_copy(kv_ref, kvs.at[c, b], loc_sem.at[0])
    kv_load.start()
    w_load = pltpu.make_async_copy(w_ref.at[:, c], ws.at[c], loc_sem.at[1])
    w_load.start()

    barrier = pltpu.get_barrier_semaphore()

    def greet(to):
        pl.semaphore_signal(barrier, inc=1, device_id=to, device_id_type=pl.DeviceIdType.MESH)

    greet(other)
    far = half // 2
    for i in (1, nz - 1):
        greet((lax.rem(z + i, nz), t, b))
    for i in range(1, X):
        greet(dev((x + i) % X, y, z, c))
    for i in range(1, Y):
        greet(dev(x, (y + i) % Y, z, c))

    enc_load.wait()
    gain_load.wait()
    enc = enc_ref[...]
    inv = lax.rsqrt(jnp.mean(enc * enc, axis=1, keepdims=True) + 1e-06)
    own_cols = []
    for s in range(nz):
        part = (enc[:, s * 256 : (s + 1) * 256] * inv) * gain_ref[:, s * 256 : (s + 1) * 256]
        lo, hi = part[:, :128], part[:, 128:]
        own_cols.append(jnp.where(c == 0, lo, hi))
        xs[:, s * 128 : (s + 1) * 128] = jnp.where(c == 0, hi, lo).astype(BF16)
    kv_load.wait()

    pl.semaphore_wait(barrier, 1 + 2 + X - 1 + Y - 1)

    send(xs, xr, x_sem.at[0], x_sem.at[1], other)
    send(kvs.at[c, b], kvs.at[c, b], kv_sem.at[0], kv_sem.at[1], other)
    npair = nz // 2
    order = [npair // 2]
    for r in range(npair // 2 - 1, 0, -1):
        order += [r, npair - r]
    order += [0]

    def pair(r):
        return lax.rem(z // 2 + r, npair)

    for r in order:
        p = pair(r)
        ds = pl.ds(2 * p, 2)
        send(w_ref.at[ds, o], ws.at[c, ds], w_ss.at[p], w_rs.at[p], other)

    fg = [(x, y), (y, x)]

    def at_xy(h, f, g):
        return (f, g) if h == 0 else (g, f)

    def slot(h, f, g):
        x_, y_ = at_xy(h, f, g)
        return mem.at[h, y_ % 2, x_, y_ // 2]

    def place(h, f, g):
        x_, y_ = at_xy(h, f, g)
        return dev(x_, y_, z, c)

    def along_f(h, off):
        f, g = fg[h]
        s = slot(h, f, g)
        to = place(h, (f + off) % 4, g)
        send(s, s, ag_ss.at[h, off - 1], ag_rs.at[h, off - 1], to, gathers)

    def from_f(h, off):
        f, g = fg[h]
        arrived(slot(h, (f + 4 - off) % 4, g), ag_ss.at[h, off - 1], ag_rs.at[h, off - 1])

    def along_g(h, i, off):
        f, g = fg[h]
        s = slot(h, (f + i) % 4, g)
        k = 3 + 3 * i + off - 1
        send(s, s, ag_ss.at[h, k], ag_rs.at[h, k], place(h, f, (g + off) % 4), gathers)

    def from_g(h, i, off):
        f, g = fg[h]
        k = 3 + 3 * i + off - 1
        arrived(slot(h, (f + i) % 4, (g + 4 - off) % 4), ag_ss.at[h, k], ag_rs.at[h, k])

    arrived(xr, x_sem.at[0], x_sem.at[1])
    for h in range(2):
        for s in range(half):
            mine = own_cols[h * half + s]
            theirs = xr[:, (h * half + s) * 128 : (h * half + s + 1) * 128].astype(F32)
            both = jnp.concatenate(
                [jnp.where(c == 0, mine, theirs), jnp.where(c == 0, theirs, mine)], axis=0
            )
            mem[h, b, x, yh, :, s * 128 : (s + 1) * 128] = both.astype(BF16)
        if h == 0:
            for off in (1, 3, 2):
                along_f(0, off)
    along_f(1, 2)

    def gather_start():
        along_g(0, 0, 2)
        for off in (1, 3, 2):
            along_g(1, 0, off)
        for off in (1, 3):
            along_f(1, off)
            along_g(0, 0, off)

    def gather_own():
        for off in (1, 3, 2):
            from_f(0, off)
            along_g(0, (4 - off) % 4, 2)
        from_f(1, 2)
        for off in (1, 3, 2):
            along_g(1, 2, off)

    def gather_rest():
        for off in (1, 3):
            from_f(1, off)
        for i in (1, 3, 2):
            for off in (1, 3):
                along_g(0, i, off)
        for i in (1, 3):
            for off in (1, 3, 2):
                along_g(1, i, off)
        mine = kvs.at[c, b]
        send(mine, mine, kv_sem.at[2], kv_sem.at[3], dev(x, yh * 2 + (1 - b), z, c), gathers)

    def own_gathered(h):
        if h == 0:
            for i in range(4):
                from_g(0, i, 2)
        else:
            for i in (0, 2):
                for off in (1, 3, 2):
                    from_g(1, i, off)

    def rest_gathered(h):
        if h == 0:
            for i in range(4):
                for off in (1, 3):
                    from_g(0, i, off)
        else:
            for i in (1, 3):
                for off in (1, 3, 2):
                    from_g(1, i, off)

    w_load.wait()
    arrived(kvs.at[o, b], kv_sem.at[0], kv_sem.at[1])

    def term(r):
        p = pair(r)
        ds = pl.ds(2 * p, 2)
        arrived(ws.at[o, ds], w_ss.at[p], w_rs.at[p])
        out = jnp.zeros((tok, 256), F32)
        for core in range(2):
            rhs = ws[core, ds].reshape(256, ws.shape[3])
            out += lax.dot_general(kvs[core, b], rhs, NT, preferred_element_type=F32)
        out *= act
        tm[2 * p] = out[:, :128]
        tm[2 * p + 1] = out[:, 128:]

    def hop(k, started):
        for j in range(PARTS):
            for d in range(2):
                start = half if (j < PARTS // 2) == (d == 0) else half - 1
                m = start - k
                if m < 1 or (k == 0 and started != (start == half)):
                    continue
                mine = tm[lax.rem(z + (m, nz - m)[d], nz), j * sub : (j + 1) * sub]
                if k == 0:
                    src = first.at[d, j]
                    src[...] = mine.astype(BF16)
                else:
                    src = run.at[d, j, m]
                    arrived(src, z_ss.at[d, j, m], z_rs.at[d, j, m])
                    src[...] = (src[...].astype(F32) + mine).astype(BF16)
                to = dev(x, y, lax.rem(z + (1, nz - 1)[d], nz), c)
                send(src, run.at[d, j, m - 1], z_ss.at[d, j, m - 1], z_rs.at[d, j, m - 1], to)

    def terms(*rs):
        for r in rs:
            term(r)

    def say_hello():
        for i in (far, nz - far):
            to = (lax.rem(z + i, nz), t, b)
            pl.semaphore_signal(hello, inc=1, device_id=to, device_id_type=pl.DeviceIdType.MESH)

    def row_dots():
        for h in range(2):
            own_gathered(h)
        blk = tok // X
        for r in range(X):
            acc = jnp.zeros((blk, 128), F32)
            for s in range(nz):
                at = (s % half) * 128
                m = mem[s // half, b, r, :, :, at : at + 128].reshape(blk, 128)
                acc += tm[s, r * blk : (r + 1) * blk] * m.astype(F32)
            qa[r * blk : (r + 1) * blk] = acc
        total = lax.dot_general(
            jnp.ones((8, 128), F32),
            qa[...],
            NT,
            precision=lax.Precision.HIGHEST,
            preferred_element_type=F32,
        )
        hs[...] = total[:1]
        hr[z] = total[:1]
        pl.semaphore_wait(hello, 2)
        for i in (8, 7, 9, 6, 10, 5, 11, 4, 12, 3, 13, 2, 14, 1, 15):
            to = lax.rem(z + i, nz)
            send(hs, hr.at[z], h_ss.at[to], h_rs.at[z], (to, t, b))

    def kv_forward():
        got = kvs.at[c, 1 - b]
        arrived(got, kv_sem.at[2], kv_sem.at[3])
        send(got, got, kv_sem.at[4], kv_sem.at[5], other)

    outs = []

    def weight_pass(h, last):
        rep = 1 - b if last else b
        for k in range(cols // 256):
            lhs = mem[h, rep, :, :, :, k * 256 : (k + 1) * 256].reshape(tok, 256)
            part = pl.ds(h * half + 2 * k, 2)
            for side in (1, 0):
                out = lax.dot_general(
                    lhs, kvs[(c, o)[side], rep], TN, preferred_element_type=F32
                )
                out = (out * act).astype(BF16).reshape(2, 128, out.shape[1])
                if last:
                    out = (ow[side, part].astype(F32) + out.astype(F32)).astype(BF16)
                ow[side, part] = out
                n = h * (cols // 256) + k
                if last and side:
                    send(ow.at[1, part], wg_ref.at[part, c], o_sem.at[0, n], o_sem.at[1, n], other)
                elif last:
                    copy = pltpu.make_async_copy(ow.at[0, part], wg_ref.at[part, c], o_sem.at[2, n])
                    copy.start()
                    outs.append(copy)

    def own_weights():
        for h in range(2):
            weight_pass(h, False)

    def row_dot_sums():
        for i in range(1, nz):
            frm = lax.rem(z + i, nz)
            arrived(hr.at[frm], h_ss.at[frm], h_rs.at[frm])
        total = jnp.zeros((1, tok), F32)
        for i in range(nz):
            total += hr[i]
        qs[...] = total
        qr[t] = total
        for i in range(1, nt):
            to = lax.rem(t + i, nt)
            send(qs, qr.at[t], q_ss.at[to], q_rs.at[t], (z, to, b))

    term(order[0])
    hop(0, True)
    gather_start()
    terms(*order[1:3])
    hop(0, False)
    events = {
        0: [lambda: terms(*order[3:5])],
        1: [gather_own, lambda: terms(*order[5:7])],
        2: [gather_rest, lambda: terms(order[7])],
        4: [say_hello],
        5: [row_dots],
        6: [own_weights, kv_forward],
        7: [row_dot_sums],
    }
    for k in range(half):
        if k:
            hop(k, True)
        for event in events.get(k, ()):
            event()
        if k >= 2:
            flush(marks[k - 1])
        marks.append(len(sent))

    per = nt // PARTS

    def piece(i):
        return remote(gs.at[i], gr.at[t], t_ss.at[i], t_rs.at[t], (z, i, b))

    for j in range(PARTS):
        total = tm[z, j * sub : (j + 1) * sub]
        for d in range(2):
            arrived(run.at[d, j, 0], z_ss.at[d, j, 0], z_rs.at[d, j, 0])
            total += run[d, j, 0].astype(F32)
        for i in range(j * per, (j + 1) * per):
            r = (i - j * per) * rows
            gs[i] = total[r : r + rows].astype(BF16)
        for i in range(j * per, (j + 1) * per):
            pl.when(i != t)(piece(i).start)
    gr[t] = gs[t]
    arrived(kvs.at[o, 1 - b], kv_sem.at[4], kv_sem.at[5])
    for h in range(2):
        rest_gathered(h)
        weight_pass(h, True)

    for copy in gathers:
        copy.wait_send()
    flush(len(sent) - nz // 2)

    for i in range(1, nt):
        frm = lax.rem(t + i, nt)
        arrived(qr.at[frm], q_ss.at[frm], q_rs.at[frm])
    row = jnp.zeros((1, tok), F32)
    for i in range(nt):
        row += qr[i]
    mine = pl.ds(pl.multiple_of(z * 256, 256), 256)
    normed = enc_ref[:, mine] * inv
    token = lax.broadcasted_iota(jnp.int32, (rows, tok), 0) + t * rows
    here = token == lax.broadcasted_iota(jnp.int32, (rows, tok), 1)
    row_dot = jnp.sum(jnp.where(here, row, 0.0), axis=1, keepdims=True) * (1.0 / width)
    for i in range(1, nt):
        frm = lax.rem(t + i, nt)
        arrived(gr.at[frm], t_ss.at[frm], t_rs.at[frm])
    sums = [jnp.zeros((rows, 128), F32), jnp.zeros((rows, 128), F32)]
    for i in range(nt):
        sums[i % 2] += gr[i].astype(F32)
    scaled = gain_ref[:, mine] * jnp.concatenate(sums, axis=1)
    eg_ref[...] = (inv * (scaled - normed * row_dot)).astype(BF16)

    for n in range(nz // 2):
        part = pl.ds(2 * n, 2)
        arrived(wg_ref.at[part, o], o_sem.at[0, n], o_sem.at[1, n])
    for copy in outs:
        copy.wait()
    flush(len(sent))
    for i in range(nt):
        pl.when(i != t)(piece(i).wait_send)


def solution(mesh):
    nz, nt = mesh.shape["section"], mesh.shape["tensor"]

    def per_device(enc_out, gain, weights, kv_grad):
        _, rows, width = enc_out.shape
        tok, hd = kv_grad.shape[2:]
        half = nz // 2
        dma = pltpu.SemaphoreType.DMA
        wg, eg = pl.pallas_call(
            functools.partial(kernel, nz),
            out_shape=(
                jax.ShapeDtypeStruct((nz, 2, 128, hd), BF16),
                jax.ShapeDtypeStruct((rows, 256), BF16),
            ),
            in_specs=[pl.BlockSpec(memory_space=pltpu.HBM)] * 4,
            out_specs=(
                pl.BlockSpec(memory_space=pl.ANY),
                pl.BlockSpec(memory_space=pltpu.VMEM),
            ),
            scratch_shapes=[
                pltpu.VMEM((rows, width), F32),
                pltpu.VMEM((1, width), F32),
                pltpu.VMEM((rows, width // 2), BF16),
                pltpu.VMEM((rows, width // 2), BF16),
                pltpu.VMEM((2, 2, X, 2, 2 * rows, half * 128), BF16),
                pltpu.VMEM((2, 2, tok, hd), BF16),
                pltpu.VMEM((2, nz, 128, hd), BF16),
                pltpu.VMEM((nz, tok, 128), F32),
                pltpu.VMEM((2, PARTS, tok // PARTS, 128), BF16),
                pltpu.VMEM((2, PARTS, half, tok // PARTS, 128), BF16),
                pltpu.VMEM((nt, rows, 128), BF16),
                pltpu.VMEM((nt, rows, 128), BF16),
                pltpu.VMEM((tok, 128), F32),
                pltpu.VMEM((1, tok), F32),
                pltpu.VMEM((nz, 1, tok), F32),
                pltpu.VMEM((1, tok), F32),
                pltpu.VMEM((nt, 1, tok), F32),
                pltpu.VMEM((2, nz, 128, hd), BF16),
                dma((4,)),
                dma((2,)),
                dma((6,)),
                dma((nz // 2,)),
                dma((nz // 2,)),
                dma((2, 15)),
                dma((2, 15)),
                dma((2, PARTS, half)),
                dma((2, PARTS, half)),
                dma((nt,)),
                dma((nt,)),
                dma((nt,)),
                dma((nt,)),
                dma((nz,)),
                dma((nz,)),
                dma((3, nz // 2)),
                pltpu.SemaphoreType.REGULAR,
            ],
            compiler_params=pltpu.CompilerParams(
                collective_id=0, has_side_effects=True, vmem_limit_bytes=32 * 1024 * 1024
            ),
            cost_estimate=pl.CostEstimate(
                flops=6 * tok * width * hd, bytes_accessed=8 * width * hd, transcendentals=0
            ),
        )(
            *(
                pltpu.with_memory_space_constraint(a, pltpu.HBM)
                for a in (
                    enc_out[0],
                    gain.reshape(1, width),
                    weights.reshape(nz, 2, 128, hd),
                    kv_grad[0, 0],
                )
            )
        )
        return wg.reshape(1, width, hd), eg[None]

    return jax.shard_map(
        per_device,
        mesh=mesh,
        in_specs=(
            P("dp", "tensor", None),
            P(),
            P("section", None, "tensor"),
            P("section", "dp", None, "tensor"),
        ),
        out_specs=(P("section", None, "tensor"), P("dp", "tensor", "section")),
        check_vma=False,
    )
```

```python
import functools

import jax
import jax.numpy as jnp
from jax import lax
from jax.experimental import pallas as pl
from jax.experimental.pallas import tpu as pltpu
from jax.sharding import PartitionSpec as P

F32, BF16 = jnp.float32, jnp.bfloat16
X, Y = 4, 4
NT = (((1,), (1,)), ((), ()))
TN = (((0,), (0,)), ((), ()))
PARTS = 4


def kernel(
    nz,
    enc_hbm,
    gain_hbm,
    w_ref,
    kv_ref,
    wg_ref,
    eg_ref,
    enc_ref,
    gain_ref,
    xs,
    xr,
    mem,
    kvs,
    ws,
    tm,
    first,
    run,
    gs,
    gr,
    qa,
    hs,
    hr,
    qs,
    qr,
    ow,
    loc_sem,
    x_sem,
    kv_sem,
    w_ss,
    w_rs,
    ag_ss,
    ag_rs,
    z_ss,
    z_rs,
    t_ss,
    t_rs,
    q_ss,
    q_rs,
    h_ss,
    h_rs,
    o_sem,
    hello,
):
    z, t, b = lax.axis_index("section"), lax.axis_index("tensor"), lax.axis_index("dp")
    x, yh, c = t // 4, (t // 2) % 2, t % 2
    y = yh * 2 + b
    o = 1 - c
    nt = X * 4
    rows, width = enc_ref.shape
    half = nz // 2
    cols = half * 128
    tok = kvs.shape[2]
    sub = tok // PARTS
    act = (z >= nz // 4).astype(F32)

    def dev(x_, y_, z_, c_):
        return (z_, x_ * 4 + (y_ // 2) * 2 + c_, y_ % 2)

    def remote(src, dst, ss, rs, to):
        return pltpu.make_async_remote_copy(
            src_ref=src,
            dst_ref=dst,
            send_sem=ss,
            recv_sem=rs,
            device_id=to,
            device_id_type=pl.DeviceIdType.MESH,
        )

    other = dev(x, y, z, o)
    sent, gathers, marks = [], [], [0]

    def send(src, dst, ss, rs, to, copies=sent):
        copy = remote(src, dst, ss, rs, to)
        copy.start()
        copies.append(copy)

    waited = [0]

    def flush(n):
        for copy in sent[waited[0] : n]:
            copy.wait_send()
        waited[0] = n

    def arrived(dst, ss, rs):
        remote(dst, dst, ss, rs, other).wait_recv()

    enc_load = pltpu.make_async_copy(enc_hbm, enc_ref, loc_sem.at[2])
    enc_load.start()
    gain_load = pltpu.make_async_copy(gain_hbm, gain_ref, loc_sem.at[3])
    gain_load.start()
    kv_load = pltpu.make_async_copy(kv_ref, kvs.at[c, b], loc_sem.at[0])
    kv_load.start()
    w_load = pltpu.make_async_copy(w_ref.at[:, c], ws.at[c], loc_sem.at[1])
    w_load.start()

    barrier = pltpu.get_barrier_semaphore()

    def greet(to):
        pl.semaphore_signal(barrier, inc=1, device_id=to, device_id_type=pl.DeviceIdType.MESH)

    greet(other)
    far = half // 2
    for i in (1, nz - 1):
        greet((lax.rem(z + i, nz), t, b))
    for i in range(1, X):
        greet(dev((x + i) % X, y, z, c))
    for i in range(1, Y):
        greet(dev(x, (y + i) % Y, z, c))

    enc_load.wait()
    gain_load.wait()
    enc = enc_ref[...]
    inv = lax.rsqrt(jnp.mean(enc * enc, axis=1, keepdims=True) + 1e-06)
    own_cols = []
    for s in range(nz):
        part = (enc[:, s * 256 : (s + 1) * 256] * inv) * gain_ref[:, s * 256 : (s + 1) * 256]
        lo, hi = part[:, :128], part[:, 128:]
        own_cols.append(jnp.where(c == 0, lo, hi))
        xs[:, s * 128 : (s + 1) * 128] = jnp.where(c == 0, hi, lo).astype(BF16)
    kv_load.wait()

    pl.semaphore_wait(barrier, 1 + 2 + X - 1 + Y - 1)

    send(xs, xr, x_sem.at[0], x_sem.at[1], other)
    send(kvs.at[c, b], kvs.at[c, b], kv_sem.at[0], kv_sem.at[1], other)
    npair = nz // 2
    order = [npair // 2]
    for r in range(npair // 2 - 1, 0, -1):
        order += [r, npair - r]
    order += [0]

    def pair(r):
        return lax.rem(z // 2 + r, npair)

    for r in order:
        p = pair(r)
        ds = pl.ds(2 * p, 2)
        send(w_ref.at[ds, o], ws.at[c, ds], w_ss.at[p], w_rs.at[p], other)

    fg = [(x, y), (y, x)]

    def at_xy(h, f, g):
        return (f, g) if h == 0 else (g, f)

    def slot(h, f, g):
        x_, y_ = at_xy(h, f, g)
        return mem.at[h, y_ % 2, x_, y_ // 2]

    def place(h, f, g):
        x_, y_ = at_xy(h, f, g)
        return dev(x_, y_, z, c)

    def along_f(h, off):
        f, g = fg[h]
        s = slot(h, f, g)
        to = place(h, (f + off) % 4, g)
        send(s, s, ag_ss.at[h, off - 1], ag_rs.at[h, off - 1], to, gathers)

    def from_f(h, off):
        f, g = fg[h]
        arrived(slot(h, (f + 4 - off) % 4, g), ag_ss.at[h, off - 1], ag_rs.at[h, off - 1])

    def along_g(h, i, off):
        f, g = fg[h]
        s = slot(h, (f + i) % 4, g)
        k = 3 + 3 * i + off - 1
        send(s, s, ag_ss.at[h, k], ag_rs.at[h, k], place(h, f, (g + off) % 4), gathers)

    def from_g(h, i, off):
        f, g = fg[h]
        k = 3 + 3 * i + off - 1
        arrived(slot(h, (f + i) % 4, (g + 4 - off) % 4), ag_ss.at[h, k], ag_rs.at[h, k])

    arrived(xr, x_sem.at[0], x_sem.at[1])
    for h in range(2):
        for s in range(half):
            mine = own_cols[h * half + s]
            theirs = xr[:, (h * half + s) * 128 : (h * half + s + 1) * 128].astype(F32)
            both = jnp.concatenate(
                [jnp.where(c == 0, mine, theirs), jnp.where(c == 0, theirs, mine)], axis=0
            )
            mem[h, b, x, yh, :, s * 128 : (s + 1) * 128] = both.astype(BF16)
        if h == 0:
            for off in (1, 3, 2):
                along_f(0, off)
    along_f(1, 2)

    def gather_start():
        along_g(0, 0, 2)
        for off in (1, 3, 2):
            along_g(1, 0, off)
        for off in (1, 3):
            along_f(1, off)
            along_g(0, 0, off)

    def gather_own():
        for off in (1, 3, 2):
            from_f(0, off)
            along_g(0, (4 - off) % 4, 2)
        from_f(1, 2)
        for off in (1, 3, 2):
            along_g(1, 2, off)

    def gather_rest():
        for off in (1, 3):
            from_f(1, off)
        for i in (1, 3, 2):
            for off in (1, 3):
                along_g(0, i, off)
        for i in (1, 3):
            for off in (1, 3, 2):
                along_g(1, i, off)
        mine = kvs.at[c, b]
        send(mine, mine, kv_sem.at[2], kv_sem.at[3], dev(x, yh * 2 + (1 - b), z, c), gathers)

    def own_gathered(h):
        if h == 0:
            for i in range(4):
                from_g(0, i, 2)
        else:
            for i in (0, 2):
                for off in (1, 3, 2):
                    from_g(1, i, off)

    def rest_gathered(h):
        if h == 0:
            for i in range(4):
                for off in (1, 3):
                    from_g(0, i, off)
        else:
            for i in (1, 3):
                for off in (1, 3, 2):
                    from_g(1, i, off)

    w_load.wait()
    arrived(kvs.at[o, b], kv_sem.at[0], kv_sem.at[1])

    def term(r):
        p = pair(r)
        ds = pl.ds(2 * p, 2)
        arrived(ws.at[o, ds], w_ss.at[p], w_rs.at[p])
        out = jnp.zeros((tok, 256), F32)
        for core in range(2):
            rhs = ws[core, ds].reshape(256, ws.shape[3])
            out += lax.dot_general(kvs[core, b], rhs, NT, preferred_element_type=F32)
        out *= act
        tm[2 * p] = out[:, :128]
        tm[2 * p + 1] = out[:, 128:]

    def hop(k, started):
        for j in range(PARTS):
            for d in range(2):
                start = half if (j < PARTS // 2) == (d == 0) else half - 1
                m = start - k
                if m < 1 or (k == 0 and started != (start == half)):
                    continue
                mine = tm[lax.rem(z + (m, nz - m)[d], nz), j * sub : (j + 1) * sub]
                if k == 0:
                    src = first.at[d, j]
                    src[...] = mine.astype(BF16)
                else:
                    src = run.at[d, j, m]
                    arrived(src, z_ss.at[d, j, m], z_rs.at[d, j, m])
                    src[...] = (src[...].astype(F32) + mine).astype(BF16)
                to = dev(x, y, lax.rem(z + (1, nz - 1)[d], nz), c)
                send(src, run.at[d, j, m - 1], z_ss.at[d, j, m - 1], z_rs.at[d, j, m - 1], to)

    def terms(*rs):
        for r in rs:
            term(r)

    def say_hello():
        for i in (far, nz - far):
            to = (lax.rem(z + i, nz), t, b)
            pl.semaphore_signal(hello, inc=1, device_id=to, device_id_type=pl.DeviceIdType.MESH)

    def row_dots():
        for h in range(2):
            own_gathered(h)
        blk = tok // X
        for r in range(X):
            acc = jnp.zeros((blk, 128), F32)
            for s in range(nz):
                at = (s % half) * 128
                m = mem[s // half, b, r, :, :, at : at + 128].reshape(blk, 128)
                acc += tm[s, r * blk : (r + 1) * blk] * m.astype(F32)
            qa[r * blk : (r + 1) * blk] = acc
        total = lax.dot_general(
            jnp.ones((8, 128), F32),
            qa[...],
            NT,
            precision=lax.Precision.HIGHEST,
            preferred_element_type=F32,
        )
        hs[...] = total[:1]
        hr[z] = total[:1]
        pl.semaphore_wait(hello, 2)
        for i in (8, 7, 9, 6, 10, 5, 11, 4, 12, 3, 13, 2, 14, 1, 15):
            to = lax.rem(z + i, nz)
            send(hs, hr.at[z], h_ss.at[to], h_rs.at[z], (to, t, b))

    def kv_forward():
        got = kvs.at[c, 1 - b]
        arrived(got, kv_sem.at[2], kv_sem.at[3])
        send(got, got, kv_sem.at[4], kv_sem.at[5], other)

    outs = []

    def weight_pass(h, last):
        rep = 1 - b if last else b
        for k in range(cols // 256):
            lhs = mem[h, rep, :, :, :, k * 256 : (k + 1) * 256].reshape(tok, 256)
            part = pl.ds(h * half + 2 * k, 2)
            for side in (1, 0):
                out = lax.dot_general(
                    lhs, kvs[(c, o)[side], rep], TN, preferred_element_type=F32
                )
                out = (out * act).astype(BF16).reshape(2, 128, out.shape[1])
                if last:
                    out = (ow[side, part].astype(F32) + out.astype(F32)).astype(BF16)
                ow[side, part] = out
                n = h * (cols // 256) + k
                if last and side:
                    send(ow.at[1, part], wg_ref.at[part, c], o_sem.at[0, n], o_sem.at[1, n], other)
                elif last:
                    copy = pltpu.make_async_copy(ow.at[0, part], wg_ref.at[part, c], o_sem.at[2, n])
                    copy.start()
                    outs.append(copy)

    def own_weights():
        for h in range(2):
            weight_pass(h, False)

    def row_dot_sums():
        for i in range(1, nz):
            frm = lax.rem(z + i, nz)
            arrived(hr.at[frm], h_ss.at[frm], h_rs.at[frm])
        total = jnp.zeros((1, tok), F32)
        for i in range(nz):
            total += hr[i]
        qs[...] = total
        qr[t] = total
        for i in range(1, nt):
            to = lax.rem(t + i, nt)
            send(qs, qr.at[t], q_ss.at[to], q_rs.at[t], (z, to, b))

    term(order[0])
    hop(0, True)
    gather_start()
    terms(*order[1:3])
    hop(0, False)
    events = {
        0: [lambda: terms(*order[3:5])],
        1: [gather_own, lambda: terms(*order[5:7])],
        2: [gather_rest, lambda: terms(order[7])],
        4: [say_hello],
        5: [row_dots],
        6: [own_weights, kv_forward],
        7: [row_dot_sums],
    }
    for k in range(half):
        if k:
            hop(k, True)
        for event in events.get(k, ()):
            event()
        if 2 <= k < half - 1:
            flush(marks[k - 1])
        marks.append(len(sent))

    per = nt // PARTS

    def piece(i):
        return remote(gs.at[i], gr.at[t], t_ss.at[i], t_rs.at[t], (z, i, b))

    for j in range(PARTS):
        total = tm[z, j * sub : (j + 1) * sub]
        for d in range(2):
            arrived(run.at[d, j, 0], z_ss.at[d, j, 0], z_rs.at[d, j, 0])
            total += run[d, j, 0].astype(F32)
        for i in range(j * per, (j + 1) * per):
            r = (i - j * per) * rows
            gs[i] = total[r : r + rows].astype(BF16)
        for i in range(j * per, (j + 1) * per):
            pl.when(i != t)(piece(i).start)
    gr[t] = gs[t]
    arrived(kvs.at[o, 1 - b], kv_sem.at[4], kv_sem.at[5])
    for h in range(2):
        rest_gathered(h)
        weight_pass(h, True)

    for copy in gathers:
        copy.wait_send()
    flush(len(sent) - nz // 2)

    for i in range(1, nt):
        frm = lax.rem(t + i, nt)
        arrived(qr.at[frm], q_ss.at[frm], q_rs.at[frm])
    row = jnp.zeros((1, tok), F32)
    for i in range(nt):
        row += qr[i]
    mine = pl.ds(pl.multiple_of(z * 256, 256), 256)
    normed = enc_ref[:, mine] * inv
    token = lax.broadcasted_iota(jnp.int32, (rows, tok), 0) + t * rows
    here = token == lax.broadcasted_iota(jnp.int32, (rows, tok), 1)
    row_dot = jnp.sum(jnp.where(here, row, 0.0), axis=1, keepdims=True) * (1.0 / width)
    for i in range(1, nt):
        frm = lax.rem(t + i, nt)
        arrived(gr.at[frm], t_ss.at[frm], t_rs.at[frm])
    sums = [jnp.zeros((rows, 128), F32), jnp.zeros((rows, 128), F32)]
    for i in range(nt):
        sums[i % 2] += gr[i].astype(F32)
    scaled = gain_ref[:, mine] * jnp.concatenate(sums, axis=1)
    eg_ref[...] = (inv * (scaled - normed * row_dot)).astype(BF16)

    for n in range(nz // 2):
        part = pl.ds(2 * n, 2)
        arrived(wg_ref.at[part, o], o_sem.at[0, n], o_sem.at[1, n])
    for copy in outs:
        copy.wait()
    flush(len(sent))
    for i in range(nt):
        pl.when(i != t)(piece(i).wait_send)


def solution(mesh):
    nz, nt = mesh.shape["section"], mesh.shape["tensor"]

    def per_device(enc_out, gain, weights, kv_grad):
        _, rows, width = enc_out.shape
        tok, hd = kv_grad.shape[2:]
        half = nz // 2
        dma = pltpu.SemaphoreType.DMA
        wg, eg = pl.pallas_call(
            functools.partial(kernel, nz),
            out_shape=(
                jax.ShapeDtypeStruct((nz, 2, 128, hd), BF16),
                jax.ShapeDtypeStruct((rows, 256), BF16),
            ),
            in_specs=[pl.BlockSpec(memory_space=pltpu.HBM)] * 4,
            out_specs=(
                pl.BlockSpec(memory_space=pl.ANY),
                pl.BlockSpec(memory_space=pltpu.VMEM),
            ),
            scratch_shapes=[
                pltpu.VMEM((rows, width), F32),
                pltpu.VMEM((1, width), F32),
                pltpu.VMEM((rows, width // 2), BF16),
                pltpu.VMEM((rows, width // 2), BF16),
                pltpu.VMEM((2, 2, X, 2, 2 * rows, half * 128), BF16),
                pltpu.VMEM((2, 2, tok, hd), BF16),
                pltpu.VMEM((2, nz, 128, hd), BF16),
                pltpu.VMEM((nz, tok, 128), F32),
                pltpu.VMEM((2, PARTS, tok // PARTS, 128), BF16),
                pltpu.VMEM((2, PARTS, half, tok // PARTS, 128), BF16),
                pltpu.VMEM((nt, rows, 128), BF16),
                pltpu.VMEM((nt, rows, 128), BF16),
                pltpu.VMEM((tok, 128), F32),
                pltpu.VMEM((1, tok), F32),
                pltpu.VMEM((nz, 1, tok), F32),
                pltpu.VMEM((1, tok), F32),
                pltpu.VMEM((nt, 1, tok), F32),
                pltpu.VMEM((2, nz, 128, hd), BF16),
                dma((4,)),
                dma((2,)),
                dma((6,)),
                dma((nz // 2,)),
                dma((nz // 2,)),
                dma((2, 15)),
                dma((2, 15)),
                dma((2, PARTS, half)),
                dma((2, PARTS, half)),
                dma((nt,)),
                dma((nt,)),
                dma((nt,)),
                dma((nt,)),
                dma((nz,)),
                dma((nz,)),
                dma((3, nz // 2)),
                pltpu.SemaphoreType.REGULAR,
            ],
            compiler_params=pltpu.CompilerParams(
                collective_id=0, has_side_effects=True, vmem_limit_bytes=32 * 1024 * 1024
            ),
            cost_estimate=pl.CostEstimate(
                flops=6 * tok * width * hd, bytes_accessed=8 * width * hd, transcendentals=0
            ),
        )(
            *(
                pltpu.with_memory_space_constraint(a, pltpu.HBM)
                for a in (
                    enc_out[0],
                    gain.reshape(1, width),
                    weights.reshape(nz, 2, 128, hd),
                    kv_grad[0, 0],
                )
            )
        )
        return wg.reshape(1, width, hd), eg[None]

    return jax.shard_map(
        per_device,
        mesh=mesh,
        in_specs=(
            P("dp", "tensor", None),
            P(),
            P("section", None, "tensor"),
            P("section", "dp", None, "tensor"),
        ),
        out_specs=(P("section", None, "tensor"), P("dp", "tensor", "section")),
        check_vma=False,
    )
```
